256 devices in a mesh: expert: 64 (over y_lo, x, z), tensor: 4 (over y_hi, core).
Axes of the slice: x: 4, y: 4 (y_hi: 2, y_lo: 2; y = y_hi * 2 + y_lo), z: 8, core: 2. Of those that a mesh axis runs over, the one named last changes fastest.
Arguments:
- tokens: bfloat16 [8192, 4096], P('expert', 'tensor'), may hold values from -6 to 6
- residual_grad: bfloat16 [8192, 4096], P('expert', 'tensor'), may hold values from -6 to 6
- dense_hidden: bfloat16 [8192, 2560], P('expert', 'tensor'), may hold values from -6 to 6
- dense_gate: bfloat16 [4096, 2560], P('expert', 'tensor'), may hold values from -0.09375 to 0.09375
- dense_up: bfloat16 [4096, 2560], P('expert', 'tensor'), may hold values from -0.09375 to 0.09375
- expert_gate: bfloat16 [64, 4096, 2560], P('expert', None, 'tensor'), may hold values from -0.09375 to 0.09375
- expert_up: bfloat16 [64, 4096, 2560], P('expert', None, 'tensor'), may hold values from -0.09375 to 0.09375
- expert_hidden: bfloat16 [64, 320, 2560], P('expert', None, 'tensor'), may hold values from -6 to 6
- expert_ids: int32 [8192, 2], P('expert'), may hold values from 0 to 63, as said below
- slot_index: int32 [8192, 2], P('expert'), may hold values from 0 to 5, as said below
- kept_mask: int32 [8192, 2], P('expert'), may hold values from 0 to 1, as said below
- gate_weights: float32 [8192, 2], P('expert'), may hold values from 0.2 to 1
Outputs:
- input_grad: bfloat16 [8192, 4096], P('expert', 'tensor')
The draws below stay inside these ranges and needn't reach their ends.
Inputs may be any that keep to these rules, and one draw needn't show every extreme that they name: `expert_ids`: the two experts of a token differ. In every group of 128 tokens (the tokens of one index of expert) some expert is named by more than 5 assignments. `slot_index`: within a group of 128 tokens, the assignments to one expert are counted in the order of all first choices in token order, then all second choices in token order; a kept assignment's slot is the number of assignments to its expert before it, and a dropped one has 5. `kept_mask`: 1 exactly where the count in that order is below 5.
All inputs are finite; a program needn't handle non-finite values.
Results may differ from the reference program's by a relative error of at most 0.014.
Values may be sent and summed in bfloat16 or wider, within the bound.
A program may use at most 128 MiB of HBM per device.

```python
import jax
import jax.numpy as jnp
from jax import lax

D = 4096
FF = 2560
FFE = 2560
TOK = 128
EXPERTS = 64
CAP = 5
SLOTS = 320
TOKENS = 8192
N_EXPERT = 64


def group_shuffle(subkey):
    return jax.random.permutation(subkey, TOK)


def routing(key):
    subkeys = jax.random.split(key, 6)
    busiest = jax.random.randint(subkeys[0], (), 0, EXPERTS)
    relabel = jax.random.permutation(subkeys[1], jnp.arange(EXPERTS, dtype=jnp.int32))
    lowest = jnp.minimum(jax.random.randint(subkeys[2], (TOKENS,), 0, EXPERTS), jax.random.randint(subkeys[3], (TOKENS,), 0, EXPERTS))
    first_choice = relabel[lowest]
    group_keys = jax.random.split(subkeys[4], N_EXPERT)
    shuffle_rank = jax.vmap(group_shuffle)(group_keys).reshape(TOKENS)
    first_choice = jnp.where(shuffle_rank < CAP + 2, busiest, first_choice)
    second = (first_choice + 1 + jax.random.randint(subkeys[5], (TOKENS,), 0, EXPERTS - 1)) % EXPERTS
    choices = jnp.stack([first_choice, second], axis=1).astype(jnp.int32)
    arrival = choices.reshape(N_EXPERT, TOK, 2).transpose(0, 2, 1).reshape(N_EXPERT, 2 * TOK)
    onehot = (arrival[:, :, None] == jnp.arange(EXPERTS, dtype=jnp.int32)).astype(jnp.int32)
    earlier = jnp.cumsum(onehot, axis=1) - onehot
    position = jnp.sum(earlier * onehot, axis=2)
    position = position.reshape(N_EXPERT, 2, TOK).transpose(0, 2, 1).reshape(TOKENS, 2)
    kept_flag = (position < CAP).astype(jnp.int32)
    slot_value = jnp.minimum(position, CAP).astype(jnp.int32)
    return (choices, slot_value, kept_flag)


def draw_expert_ids(key, part):
    shared = routing(key)
    return shared[0]


def draw_slot_index(key, part):
    shared = routing(key)
    return shared[1]


def draw_kept_mask(key, part):
    shared = routing(key)
    return shared[2]


def shard_levels(rng, shape, pieces, low, top_value):
    factor_of, own = 1.0, jax.random.fold_in(rng, 6)
    for dim, parts in pieces:
        steps = jnp.exp(jax.random.uniform(jax.random.fold_in(own, dim), (parts,), jnp.float32, low / len(pieces), top_value / len(pieces)))
        factor_of = factor_of * jnp.repeat(steps, shape[dim] // parts).reshape([-1 if axis == dim else 1 for axis in range(len(shape))])
    return factor_of


def bell_draw(own_key, extent, scale, bound, cuts=(), kind=jnp.bfloat16):
    array = jax.random.normal(own_key, extent, jnp.float32) * scale
    if len(cuts) > 0:
        array = shard_levels(own_key, extent, cuts, -0.22, 0.18) * array
    return jnp.clip(array, min=-bound, max=bound).astype(kind)


def setup_inputs(seed: int = 0) -> dict:
    key_list = jax.random.split(jax.random.key(seed), 13)
    tokens = bell_draw(key_list[0], (TOKENS, D), 1.0, 6.0, ((0, 64), (1, 4)))
    residual_grad = bell_draw(key_list[1], (TOKENS, D), 1.0, 6.0, ((0, 64), (1, 4)))
    dense_hidden = bell_draw(key_list[2], (TOKENS, FF), 1.0, 6.0, ((0, 64), (1, 4)))
    dense_gate = bell_draw(key_list[3], (D, FF), D ** -0.5, 0.09375, ((0, 64), (1, 4)))
    dense_up = bell_draw(key_list[4], (D, FF), D ** -0.5, 0.09375, ((0, 64), (1, 4)))
    expert_gate = bell_draw(key_list[5], (EXPERTS, D, FFE), D ** -0.5, 0.09375, ((0, 64), (2, 4)))
    expert_up = bell_draw(key_list[6], (EXPERTS, D, FFE), D ** -0.5, 0.09375, ((0, 64), (2, 4)))
    expert_hidden = bell_draw(key_list[7], (EXPERTS, SLOTS, FFE), 1.0, 6.0, ((0, 64), (2, 4)))
    expert_ids = draw_expert_ids(jax.random.fold_in(key_list[12], 71), 0)
    slot_index = draw_slot_index(jax.random.fold_in(key_list[12], 71), 0)
    kept_mask = draw_kept_mask(jax.random.fold_in(key_list[12], 71), 0)
    gate_weights = jnp.clip(0.2 + 0.8 * jax.random.uniform(key_list[11], (TOKENS, 2), jnp.float32) ** shard_levels(key_list[11], (TOKENS, 2), ((0, 64),), -0.2, 0.2), 0.2, 1.0)
    return dict(tokens=tokens, residual_grad=residual_grad, dense_hidden=dense_hidden, dense_gate=dense_gate, dense_up=dense_up, expert_gate=expert_gate, expert_up=expert_up, expert_hidden=expert_hidden, expert_ids=expert_ids, slot_index=slot_index, kept_mask=kept_mask, gate_weights=gate_weights)


def swiglu_back(inputs, gate_matrix, up_matrix, hidden_grad):
    pre_gate = jnp.dot(inputs, gate_matrix, preferred_element_type=jnp.float32)
    pre_up = jnp.dot(inputs, up_matrix, preferred_element_type=jnp.float32)
    upstream = hidden_grad.astype(jnp.float32)
    sigmoid_gate = jax.nn.sigmoid(pre_gate)
    gate_back = (upstream * pre_up * sigmoid_gate * (1.0 + pre_gate * (1.0 - sigmoid_gate))).astype(jnp.bfloat16)
    up_back = (upstream * pre_gate * sigmoid_gate).astype(jnp.bfloat16)
    return jnp.dot(gate_back, gate_matrix.T, preferred_element_type=jnp.float32) + jnp.dot(up_back, up_matrix.T, preferred_element_type=jnp.float32)


def one_expert(inputs):
    expert_rows, gate_matrix, up_matrix, hidden_grad = inputs
    return swiglu_back(expert_rows, gate_matrix, up_matrix, hidden_grad)


def reference(tokens, residual_grad, dense_hidden, dense_gate, dense_up, expert_gate, expert_up, expert_hidden, expert_ids, slot_index, kept_mask, gate_weights):
    dense_back = swiglu_back(tokens, dense_gate, dense_up, dense_hidden)
    take_mask = (kept_mask == 1) & (slot_index < CAP)
    group_of = (jnp.arange(TOKENS, dtype=jnp.int32) // TOK)[:, None]
    row_index = expert_ids * SLOTS + group_of * CAP + slot_index
    flat_slot = jnp.where(take_mask, row_index, EXPERTS * SLOTS).astype(jnp.int32)
    spread = jnp.broadcast_to(tokens[:, None, :], (TOKENS, 2, D)).reshape(TOKENS * 2, D)
    expert_input = jnp.zeros((EXPERTS * SLOTS, D), jnp.bfloat16).at[flat_slot.reshape(-1)].add(spread, mode="drop")
    expert_back = lax.map(one_expert, (expert_input.reshape(EXPERTS, SLOTS, D), expert_gate, expert_up, expert_hidden))
    expert_back = expert_back.reshape(EXPERTS * SLOTS, D)
    picked = expert_back[jnp.minimum(flat_slot, EXPERTS * SLOTS - 1)]
    weights = jnp.where(take_mask, gate_weights, 0.0).astype(jnp.float32)
    moe_back = jnp.sum(picked * weights[:, :, None], axis=1)
    return (residual_grad.astype(jnp.float32) + dense_back + moe_back).astype(jnp.bfloat16)
```

```python
import functools

import jax
import jax.numpy as jnp
import numpy as np
from jax import lax
from jax.experimental import pallas as pl
from jax.experimental.pallas import tpu as pltpu
from jax.sharding import PartitionSpec as P

MESH = pl.DeviceIdType.MESH
F32, BF16 = jnp.float32, jnp.bfloat16

X, Z = 4, 8
CAP = 5
CHUNKS = 1


def sizes():
    experts = 2 * X * Z
    return experts, experts * CAP, 4 * CAP, X * Z * 4 * CAP


def tables():
    experts, slots, quad, rows = sizes()
    keys = np.zeros((rows,), np.float32)
    first = np.zeros((rows, rows), np.float32)
    second = np.zeros((rows, rows), np.float32)
    for x in range(X):
        for z in range(Z):
            for g in range(2):
                for e in range(2):
                    for s in range(CAP):
                        q = (g * 2 + e) * CAP + s
                        by_xz = (x * Z + z) * quad + q
                        by_zx = (z * X + x) * quad + q
                        keys[by_xz] = g * slots + (e * X * Z + x * Z + z) * CAP + s
                        first[by_zx, by_xz] = 1.0
                        second[e * slots + (g * X * Z + x * Z + z) * CAP + s, by_zx] = 1.0
    key_sub = np.broadcast_to(keys[:, None], (rows, 128)).astype(np.float32)
    key_lane = np.broadcast_to(keys[None, :], (8, rows)).astype(np.float32)
    perms = np.stack([first, second, second.T, first.T])
    return key_sub, key_lane, perms


def backs(gate, up, upstream):
    s = jax.nn.sigmoid(gate)
    weighted = upstream * s
    return weighted * up * (1.0 + gate * (1.0 - s)), weighted * gate


def nt(a, b):
    return lax.dot_general(a, b, (((1,), (1,)), ((), ())), preferred_element_type=F32)


def dot(a, b):
    return jnp.dot(a, b, preferred_element_type=F32)


def kernel(
    tok, route, wsplit, hid, eg, eu, eh, res, key_sub, key_lane, perms_in,
    out,
    T, RT, H, Wd, Wx, perms, S, B1, B1p, B2, B2p, Xe, Eback, Esib_s, Esib_r, Ex_s, Ex_r, Rb, R2, ZB, ZBp, XB,
    Dback, Dsib_s, Dsib_r, Dx_s, Dx_r, Down, Fin, Fs, Fr,
    send, recv, local,
):
    experts, slots, quad, rows = sizes()
    n_tok, dq = tok.shape
    db = dq // 2
    dc = db // CHUNKS
    rb = wsplit.shape[1]
    e = lax.axis_index("expert")
    t = lax.axis_index("tensor")
    yl, x, z = e // (X * Z), lax.rem(e // Z, X), lax.rem(e, Z)
    yh, c = t // 2, lax.rem(t, 2)

    def dev(yl_, x_, z_, yh_, c_):
        return (yl_ * (X * Z) + x_ * Z + z_, yh_ * 2 + c_)

    def colblk(yl_, yh_, c_):
        return pl.multiple_of((yh_ * 2 + c_) * dq + yl_ * db, db)

    def xr(d):
        return lax.rem(x + d, X)

    def zr(d):
        return lax.rem(z + d + Z, Z)

    partner = dev(1 - yl, x, z, yh, c)
    sibling = dev(yl, x, z, yh, 1 - c)
    others = [(1, 0), (1, 1), (0, 1)]

    def chip(dyl, dyh):
        return (1 - yl if dyl else yl), (1 - yh if dyh else yh)

    pending = []

    def push(src, dst, device):
        i = len(pending)
        copy = pltpu.make_async_remote_copy(
            src_ref=src, dst_ref=dst, send_sem=send.at[i], recv_sem=recv.at[i],
            device_id=device, device_id_type=MESH,
        )
        copy.start()
        pending.append(copy)
        return copy

    locals_ = []

    def load(src, dst):
        copy = pltpu.make_async_copy(src, dst, local.at[len(locals_)])
        copy.start()
        locals_.append(copy)
        return copy

    perm_loads = [load(perms_in, perms)]
    weight_loads = []
    n_tiles = eg.shape[1] // 128
    for j in range(n_tiles):
        weight_loads.append(load(eg.at[:, pl.ds(j * 128, 128)], Wx.at[:, pl.ds(j * 256, 128)]))
        weight_loads.append(load(eu.at[:, pl.ds(j * 128, 128)], Wx.at[:, pl.ds(j * 256 + 128, 128)]))

    barrier = pltpu.get_barrier_semaphore()
    peers = [dev(yl_, x, z, yh_, c_) for dyl, dyh in others for yl_, yh_ in [chip(dyl, dyh)] for c_ in (c, 1 - c)]
    peers += [sibling]
    peers += [dev(yl, xr(d), z, yh, c) for d in range(1, X)]
    peers += [dev(yl, x, zr(d), yh, c) for d in range(1, Z)]
    for peer in peers:
        pl.semaphore_signal(barrier, inc=1, device_id=peer, device_id_type=MESH)
    pl.semaphore_wait(barrier, len(peers))

    my_cols = pl.multiple_of(t * dq, dq)
    own_half = pl.multiple_of(yl * db, db)
    oth_half = pl.multiple_of((1 - yl) * db, db)
    sw_route = push(route, RT.at[yl], partner)
    sw_tok = push(tok.at[:, pl.ds(oth_half, db)], T.at[yl, :, pl.ds(my_cols + oth_half, db)], partner)
    sw_w = push(wsplit.at[1 - yl], Wd.at[yl, x, z], partner)
    sw_h = push(hid.at[1 - yl], H.at[yl], partner)

    RT[yl] = route[...]
    T[yl, :, pl.ds(my_cols, dq)] = tok[...]
    Wd[yl, x, z] = wsplit[yl]
    H[yl] = hid[yl]

    sw_route.wait_recv()
    picks = []
    for g in range(2):
        codes = RT[g]
        hit = (key_sub[...] == codes[0:1, :] + g * slots) | (key_sub[...] == codes[1:2, :] + g * slots)
        picks.append(jnp.where(hit, 1.0, 0.0).astype(BF16))
    sw_tok.wait_recv()
    mine = colblk(yl, yh, c)
    x_copies = []
    for h in range(CHUNKS):
        lanes = pl.ds(pl.multiple_of(mine + h * dc, dc), dc)
        packed = (dot(picks[0], T[0, :, lanes]) + dot(picks[1], T[1, :, lanes])).astype(BF16)
        S[h] = packed.reshape(X, Z * quad, dc)
        for d in (1, X - 1, *range(2, X - 1)) if X > 2 else (1,):
            x_copies.append(push(S.at[h, xr(d)], B1.at[h, x], dev(yl, xr(d), z, yh, c)))
        B1[h, x] = S[h, x]

    t_first = [push(tok.at[:, pl.ds(own_half, db)], T.at[yl, :, pl.ds(my_cols + own_half, db)], partner)]
    t_sib = [push(tok, T.at[yl, :, pl.ds(my_cols, dq)], sibling)]
    for dyl, dyh in others[1:]:
        yl_, yh_ = chip(dyl, dyh)
        t_first.append(push(tok, T.at[yl, :, pl.ds(my_cols, dq)], dev(yl_, x, z, yh_, c)))

    fwd_steps, bwd_steps = Z // 2, (Z - 1) // 2
    a_fwd, a_bwd, a_x, b_x, b_fwd, b_bwd = [], [], [], [], [], []
    z_next, z_prev = dev(yl, x, zr(1), yh, c), dev(yl, x, zr(-1), yh, c)

    def a_spread(zz):
        for d in range(1, X):
            a_x.append(push(Wd.at[0, x, zz], Wd.at[0, x, zz], dev(yl, xr(d), z, yh, c)))

    def ag_start():
        sw_w.wait_recv()
        for d in range(1, X):
            b_x.append(push(Wd.at[1, x, z], Wd.at[1, x, z], dev(yl, xr(d), z, yh, c)))
        a_fwd.append(push(Wd.at[0, x, z], Wd.at[0, x, z], z_next))
        if bwd_steps:
            a_bwd.append(push(Wd.at[0, x, z], Wd.at[0, x, z], z_prev))
        a_spread(z)

    def b_start():
        for copy in b_x:
            copy.wait_recv()
        b_fwd.append(push(Wd.at[1, :, z], Wd.at[1, :, z], z_next))
        if bwd_steps:
            b_bwd.append(push(Wd.at[1, :, z], Wd.at[1, :, z], z_prev))

    def a_step(s):
        def run():
            a_fwd[s - 1].wait_recv()
            zz = zr(-s)
            if s < fwd_steps:
                a_fwd.append(push(Wd.at[0, x, zz], Wd.at[0, x, zz], z_next))
            a_spread(zz)
            if s <= bwd_steps:
                a_bwd[s - 1].wait_recv()
                zz = zr(s)
                if s < bwd_steps:
                    a_bwd.append(push(Wd.at[0, x, zz], Wd.at[0, x, zz], z_prev))
                a_spread(zz)
        return run

    def b_step(s):
        def run():
            b_fwd[s - 1].wait_recv()
            if s < fwd_steps:
                zz = zr(-s)
                b_fwd.append(push(Wd.at[1, :, zz], Wd.at[1, :, zz], z_next))
            if s <= bwd_steps:
                b_bwd[s - 1].wait_recv()
                if s < bwd_steps:
                    zz = zr(s)
                    b_bwd.append(push(Wd.at[1, :, zz], Wd.at[1, :, zz], z_prev))
        return run

    ag_tasks = [ag_start, b_start]
    for s in range(1, fwd_steps + 1):
        ag_tasks += [a_step(s), b_step(s)]

    def service(n=1):
        for _ in range(n):
            if ag_tasks:
                ag_tasks.pop(0)()

    for load_ in perm_loads:
        load_.wait()
    z_order = sorted(range(1, Z), key=lambda d: -min(d, Z - d))
    z_copies = []
    for h in range(CHUNKS):
        for copy in x_copies[h * (X - 1):(h + 1) * (X - 1)]:
            copy.wait_recv()
        B1p[h] = dot(perms[0], B1[h].reshape(rows, dc)).astype(BF16).reshape(Z, X * quad, dc)
        for d in z_order:
            z_copies.append(push(B1p.at[h, zr(d)], B2.at[h, z], dev(yl, x, zr(d), yh, c)))
        B2[h, z] = B1p[h, z]

    service(1)
    for (dyl, dyh), copy in zip(others, t_first):
        copy.wait_recv()
        yl_, yh_ = chip(dyl, dyh)
        cols = pl.ds(pl.multiple_of((yh_ * 2 + c) * dq, dq), dq)
        t_sib.append(push(T.at[yl_, :, cols], T.at[yl_, :, cols], sibling))
    service(1)

    y_copies, y_sib = [], []
    for h in range(CHUNKS):
        for copy in z_copies[h * (Z - 1):(h + 1) * (Z - 1)]:
            copy.wait_recv()
        B2p[h] = dot(perms[1], B2[h].reshape(rows, dc)).astype(BF16).reshape(2, slots, dc)
        here = pl.ds(pl.multiple_of(mine + h * dc, dc), dc)
        for dyl, dyh in (others[2], others[0], others[1]):
            yl_, yh_ = chip(dyl, dyh)
            y_copies.append(((dyl, dyh), push(B2p.at[h, yl_], Xe.at[:, here], dev(yl_, x, z, yh_, c))))
        y_sib.append(push(B2p.at[h, yl], Xe.at[:, here], sibling))
        Xe[:, here] = B2p[h, yl]
    service(2)
    for i, ((dyl, dyh), copy) in enumerate(y_copies):
        h = i // 3
        copy.wait_recv()
        yl_, yh_ = chip(dyl, dyh)
        cols = pl.ds(pl.multiple_of(colblk(yl_, yh_, c) + h * dc, dc), dc)
        y_sib.append(push(Xe.at[:, cols], Xe.at[:, cols], sibling))
        service(1)
    for copy in weight_loads:
        copy.wait()
    for copy in y_sib:
        copy.wait_recv()

    for j in range(n_tiles):
        pre = dot(Xe[...], Wx[:, pl.ds(j * 256, 256)])
        upstream = eh[:, pl.ds(j * 128, 128)].astype(F32)
        gate_back, up_back = backs(pre[:, :128], pre[:, 128:], upstream)
        Eback[:, pl.ds(j * 256, 128)] = gate_back.astype(BF16)
        Eback[:, pl.ds(j * 256 + 128, 128)] = up_back.astype(BF16)
        service(1)

    targets = [(0, 1), (1, 0), (1, 1), (0, 0)]
    e_sib, e_x = {}, {}
    for h in range(CHUNKS):
        for i, (dyl, dyh) in enumerate(targets):
            yl_, yh_ = chip(dyl, dyh)
            r0 = pl.multiple_of(colblk(yl_, yh_, 1 - c) + h * dc, dc)
            Esib_s[h, i] = nt(Eback[...], Wx[pl.ds(r0, dc), :]).astype(BF16)
            e_sib[h, i] = push(Esib_s.at[h, i], Esib_r.at[h, i], sibling)
        for i, (dyl, dyh) in enumerate(targets):
            yl_, yh_ = chip(dyl, dyh)
            r0 = pl.multiple_of(colblk(yl_, yh_, c) + h * dc, dc)
            part = nt(Eback[...], Wx[pl.ds(r0, dc), :])
            e_sib[h, i].wait_recv()
            total = part + Esib_r[h, i].astype(F32)
            if i < 3:
                Ex_s[h, i] = total.astype(BF16)
                e_x[h, i] = push(Ex_s.at[h, i], Ex_r.at[h, i], dev(yl_, x, z, yh_, c))
            else:
                Rb[h] = total

    service(len(ag_tasks))
    sw_h.wait_recv()
    for copy in t_sib:
        copy.wait_recv()
    for copy in a_x:
        copy.wait_recv()
    tokens = T[...].reshape(2 * n_tok, T.shape[2])
    for j in range(2):
        w = Wd[:, :, :, :, pl.ds(j * 256, 256)].reshape(Wd.shape[0] * X * Z * rb, 256)
        pre = dot(tokens, w)
        upstream = H[:, :, pl.ds(j * 128, 128)].reshape(2 * n_tok, 128).astype(F32)
        gate_back, up_back = backs(pre[:, :128], pre[:, 128:], upstream)
        Dback[:, pl.ds(j * 256, 128)] = gate_back.astype(BF16)
        Dback[:, pl.ds(j * 256 + 128, 128)] = up_back.astype(BF16)
    w = Wd[:, :, :, :, pl.ds(512, 128)].reshape(Wd.shape[0] * X * Z * rb, 128)
    pre = dot(tokens, w)
    turned = pltpu.roll(pre, 64, axis=1)
    low = lax.broadcasted_iota(jnp.int32, pre.shape, 1) < 64
    upstream = H[:, :, pl.ds(256, 128)].reshape(2 * n_tok, 128).astype(F32)
    gate_back, up_back = backs(jnp.where(low, pre, turned), jnp.where(low, turned, pre), upstream)
    Dback[:, pl.ds(512, 128)] = jnp.where(low, gate_back, up_back).astype(BF16)

    blocks_per = db // rb

    def dense_rows(yl_, yh_, c_):
        first = ((yh_ * 2 + c_) * 2 + yl_) * blocks_per
        return Wf(first)

    def Wf(first):
        yy, rest = first // (X * Z), lax.rem(first, X * Z)
        xx, zz = rest // Z, lax.rem(rest, Z)
        return Wd[yy, xx, pl.ds(zz, blocks_per)].reshape(db, Wd.shape[4])

    d_sib, d_x = {}, {}
    for i, (dyl, dyh) in enumerate(targets):
        yl_, yh_ = chip(dyl, dyh)
        Dsib_s[i] = nt(Dback[...], dense_rows(yl_, yh_, 1 - c)).astype(BF16)
        d_sib[i] = push(Dsib_s.at[i], Dsib_r.at[i], sibling)
    for i, (dyl, dyh) in enumerate(targets):
        yl_, yh_ = chip(dyl, dyh)
        part = nt(Dback[...], dense_rows(yl_, yh_, c))
        d_sib[i].wait_recv()
        total = part + Dsib_r[i].astype(F32)
        if i < 3:
            Dx_s[i] = total.astype(BF16)
            d_x[i] = push(Dx_s.at[i], Dx_r.at[i], dev(yl_, x, z, yh_, c))
        else:
            Down[...] = total

    zb, xb = [], []
    for h in range(CHUNKS):
        for i in range(3):
            e_x[h, i].wait_recv()
        R2[h, yl] = (Rb[h] + Ex_r[h, 0].astype(F32)).astype(BF16)
        R2[h, 1 - yl] = (Ex_r[h, 1].astype(F32) + Ex_r[h, 2].astype(F32)).astype(BF16)
        B1p2 = dot(perms[2], R2[h].reshape(rows, dc)).astype(BF16).reshape(Z, X * quad, dc)
        B2[h] = B1p2
        for d in z_order:
            zb.append(push(B2.at[h, zr(d)], ZB.at[h, z], dev(yl, x, zr(d), yh, c)))
        ZB[h, z] = B2[h, z]
    for h in range(CHUNKS):
        for copy in zb[h * (Z - 1):(h + 1) * (Z - 1)]:
            copy.wait_recv()
        ZBp[h] = dot(perms[3], ZB[h].reshape(rows, dc)).astype(BF16).reshape(X, Z * quad, dc)
        for d in (1, X - 1, *range(2, X - 1)) if X > 2 else (1,):
            xb.append(push(ZBp.at[h, xr(d)], XB.at[h, x], dev(yl, xr(d), z, yh, c)))
        XB[h, x] = ZBp[h, x]

    for i in range(3):
        d_x[i].wait_recv()
    Fin[...] = Down[...] + Dx_r[0].astype(F32) + Dx_r[1].astype(F32) + Dx_r[2].astype(F32)
    picks = []
    for g in range(2):
        codes = jnp.concatenate([RT[g], jnp.zeros((120, 128), F32)], axis=0).T
        picks.append(
            [
                (
                    jnp.where(key_lane[0:1, :] == codes[:, k:k + 1] + g * slots, 1.0, 0.0).astype(BF16),
                    codes[:, 2 + k:3 + k],
                )
                for k in range(2)
            ]
        )
    for h in range(CHUNKS):
        for copy in xb[h * (X - 1):(h + 1) * (X - 1)]:
            copy.wait_recv()
        returned = XB[h].reshape(rows, dc)
        for g in range(2):
            total = Fin[pl.ds(g * n_tok, n_tok), pl.ds(h * dc, dc)]
            for hot, weight in picks[g]:
                total = total + weight * dot(hot, returned)
            Fin[pl.ds(g * n_tok, n_tok), pl.ds(h * dc, dc)] = total
    own_rows = pl.ds(pl.multiple_of(yl * n_tok, n_tok), n_tok)
    oth_rows = pl.ds(pl.multiple_of((1 - yl) * n_tok, n_tok), n_tok)
    Fs[...] = Fin[oth_rows, :].astype(BF16)
    last = push(Fs, Fr, partner)
    out[:, pl.ds(own_half, db)] = (res[:, pl.ds(own_half, db)].astype(F32) + Fin[own_rows, :]).astype(BF16)
    last.wait_recv()
    out[:, pl.ds(oth_half, db)] = (res[:, pl.ds(oth_half, db)].astype(F32) + Fr[...].astype(F32)).astype(BF16)
    for copy in pending:
        copy.wait_send()


N_SEMS = 140


def run_kernel(tok, route, wsplit, hid, eg, eu, eh, res):
    experts, slots, quad, rows = sizes()
    n_tok, dq = tok.shape
    d = dq * 4
    db = dq // 2
    dc = db // CHUNKS
    rb = wsplit.shape[1]
    key_sub, key_lane, perms = tables()
    vm = pl.BlockSpec(memory_space=pltpu.VMEM)
    hbm = pl.BlockSpec(memory_space=pl.ANY)
    V = pltpu.VMEM
    C = CHUNKS
    wide = eg.shape[1] * 2
    return pl.pallas_call(
        kernel,
        out_shape=jax.ShapeDtypeStruct((n_tok, dq), BF16),
        in_specs=[vm, vm, vm, vm, hbm, hbm, vm, vm, vm, vm, hbm],
        out_specs=vm,
        scratch_shapes=[
            V((2, n_tok, d), BF16),
            V((2, 8, 128), F32),
            V((2, n_tok, 384), BF16),
            V((2, X, Z, rb, 640), BF16),
            V((d, wide), BF16),
            V((4, rows, rows), BF16),
            V((C, X, Z * quad, dc), BF16),
            V((C, X, Z * quad, dc), BF16),
            V((C, Z, X * quad, dc), BF16),
            V((C, Z, X * quad, dc), BF16),
            V((C, 2, slots, dc), BF16),
            V((slots, d), BF16),
            V((slots, wide), BF16),
            V((C, 4, slots, dc), BF16),
            V((C, 4, slots, dc), BF16),
            V((C, 3, slots, dc), BF16),
            V((C, 3, slots, dc), BF16),
            V((C, slots, dc), F32),
            V((C, 2, slots, dc), BF16),
            V((C, Z, X * quad, dc), BF16),
            V((C, X, Z * quad, dc), BF16),
            V((C, X, Z * quad, dc), BF16),
            V((2 * n_tok, 640), BF16),
            V((4, 2 * n_tok, db), BF16),
            V((4, 2 * n_tok, db), BF16),
            V((3, 2 * n_tok, db), BF16),
            V((3, 2 * n_tok, db), BF16),
            V((2 * n_tok, db), F32),
            V((2 * n_tok, db), F32),
            V((n_tok, db), BF16),
            V((n_tok, db), BF16),
            pltpu.SemaphoreType.DMA((N_SEMS,)),
            pltpu.SemaphoreType.DMA((N_SEMS,)),
            pltpu.SemaphoreType.DMA((16,)),
        ],
        compiler_params=pltpu.CompilerParams(
            collective_id=0, has_side_effects=True, vmem_limit_bytes=60 * 1024 * 1024
        ),
    )(
        tok, route, wsplit, hid, eg, eu, eh, res,
        jnp.asarray(key_sub), jnp.asarray(key_lane), jnp.asarray(perms, BF16),
    )


def body(
    tokens,
    residual_grad,
    dense_hidden,
    dense_gate,
    dense_up,
    expert_gate,
    expert_up,
    expert_hidden,
    expert_ids,
    slot_index,
    kept_mask,
    gate_weights,
):
    take = (kept_mask == 1) & (slot_index < CAP)
    code = jnp.where(take, expert_ids * CAP + slot_index, -100000).astype(F32)
    weight = jnp.where(take, gate_weights, 0.0)
    route = jnp.concatenate([code, weight, jnp.zeros((code.shape[0], 4), F32)], axis=1).T
    halves, hidden = [], []
    for h in range(2):
        o = h * 320
        halves.append(
            jnp.concatenate(
                [
                    dense_gate[:, o:o + 128], dense_up[:, o:o + 128],
                    dense_gate[:, o + 128:o + 256], dense_up[:, o + 128:o + 256],
                    dense_gate[:, o + 256:o + 320], dense_up[:, o + 256:o + 320],
                ],
                axis=1,
            )
        )
        hidden.append(
            jnp.concatenate([dense_hidden[:, o:o + 320], dense_hidden[:, o + 256:o + 320]], axis=1)
        )
    return run_kernel(
        tokens, route, jnp.stack(halves), jnp.stack(hidden),
        expert_gate[0], expert_up[0], expert_hidden[0], residual_grad,
    )


def solution(mesh):
    both = P("expert", "tensor")
    rows = P("expert", None)
    last = P("expert", None, "tensor")
    placed = (both, both, both, both, both, last, last, last, rows, rows, rows, rows)
    return jax.shard_map(body, mesh=mesh, in_specs=placed, out_specs=both, check_vma=False)
```

```python
import functools

import jax
import jax.numpy as jnp
import numpy as np
from jax import lax
from jax.experimental import pallas as pl
from jax.experimental.pallas import tpu as pltpu
from jax.sharding import PartitionSpec as P

MESH = pl.DeviceIdType.MESH
F32, BF16 = jnp.float32, jnp.bfloat16

X, Z = 4, 8
CAP = 5
CHUNKS = 2


def sizes():
    experts = 2 * X * Z
    return experts, experts * CAP, 2 * CAP, 2 * experts * CAP


def tables():
    experts, slots, ten, rows = sizes()
    keys = np.zeros((rows,), np.float32)
    first = np.zeros((rows, rows), np.float32)
    second = np.zeros((rows, rows), np.float32)
    for x in range(X):
        for z in range(Z):
            for e in range(2):
                for s in range(CAP):
                    by_xz = (x * Z + z) * ten + e * CAP + s
                    keys[by_xz] = (e * X * Z + x * Z + z) * CAP + s
                    for half in range(2):
                        by_zx = (z * 2 + half) * X * ten + x * ten + e * CAP + s
                        first[by_zx, half * slots + by_xz] = 1.0
                        second[half * slots + e * (slots // 2) + (x * Z + z) * CAP + s, by_zx] = 1.0
    columns = np.zeros((rows, 128), np.float32)
    columns[:, 0] = keys
    for k, order in enumerate((first, second, second.T, first.T)):
        columns[:, 1 + k] = np.argmax(order, axis=1)
    key_lane = np.broadcast_to(keys[None, :slots], (8, slots)).astype(np.float32)
    return columns, key_lane


def backs(gate, up, upstream):
    s = jax.nn.sigmoid(gate)
    weighted = upstream * s
    return weighted * up * (1.0 + gate * (1.0 - s)), weighted * gate


def nt(a, b):
    return lax.dot_general(a, b, (((1,), (1,)), ((), ())), preferred_element_type=F32)


def dot(a, b):
    return jnp.dot(a, b, preferred_element_type=F32)


def stack(v):
    w = v.shape[1] // 2
    return jnp.concatenate([v[:, :w], v[:, w:]], axis=0)


def spread(v):
    n = v.shape[0] // 2
    return jnp.concatenate([v[:n], v[n:]], axis=1)


def kernel(
    tok, ids, slot, kept, gate_w, dg, du, dh, eg, eu, eh, res, table, key_lane,
    out,
    T, Ws, Hs, H, Wd, Wx, perms, S, B1, B1p, B2, B2p, Xe, Epre, Eback, Esib_s, Esib_r, Ex_s, Ex_r, Etot, R2,
    Z2, ZB, ZBp, XB, Dback, Dsib_s, Dsib_r, Dx_s, Dx_r, Dtot,
    send, recv, local,
):
    experts, slots, ten, rows = sizes()
    half = slots // 2
    n_tok, dq = tok.shape
    dc = dq // CHUNKS
    w = dc // 2
    rb = dg.shape[0]
    e = lax.axis_index("expert")
    t = lax.axis_index("tensor")
    yl, x, z = e // (X * Z), lax.rem(e // Z, X), lax.rem(e, Z)
    yh, c = t // 2, lax.rem(t, 2)

    def dev(yl_, x_, z_, yh_, c_):
        return (yl_ * (X * Z) + x_ * Z + z_, yh_ * 2 + c_)

    def lanes(t_, width):
        return pl.ds(pl.multiple_of(t_ * width, width), width)

    def xr(d):
        return lax.rem(x + d, X)

    def zr(d):
        return lax.rem(z + d + Z, Z)

    partner = dev(1 - yl, x, z, yh, c)
    sibling = dev(yl, x, z, yh, 1 - c)
    others = [(0, 1), (1, 0), (1, 1)]

    def chip(dyl, dyh):
        return (1 - yl if dyl else yl), (1 - yh if dyh else yh)

    pending = []

    def push(src, dst, device):
        i = len(pending)
        copy = pltpu.make_async_remote_copy(
            src_ref=src, dst_ref=dst, send_sem=send.at[i], recv_sem=recv.at[i],
            device_id=device, device_id_type=MESH,
        )
        copy.start()
        pending.append(copy)
        return copy

    locals_ = []

    def load(src, dst):
        copy = pltpu.make_async_copy(src, dst, local.at[len(locals_)])
        copy.start()
        locals_.append(copy)
        return copy

    barrier = pltpu.get_barrier_semaphore()
    peers = [dev(yl, xr(d), z, yh, c) for d in range(1, X)]
    peers += [dev(yl, x, zr(d), yh, c) for d in range(1, Z)]
    for dyl, dyh in others:
        yl_, yh_ = chip(dyl, dyh)
        peers += [dev(yl_, x, z, yh_, c)]
    peers += [sibling]
    for peer in peers:
        pl.semaphore_signal(barrier, inc=1, device_id=peer, device_id_type=MESH)

    weight_loads = []
    n_tiles = eg.shape[3] // 128
    for j in range(n_tiles):
        weight_loads.append(load(eg.at[:, :, :, pl.ds(j * 128, 128)], Wx.at[:, :, :, pl.ds(j * 256, 128)]))
        weight_loads.append(load(eu.at[:, :, :, pl.ds(j * 128, 128)], Wx.at[:, :, :, pl.ds(j * 256 + 128, 128)]))

    take = (kept[...] == 1) & (slot[...] < CAP)
    code = jnp.where(take, ids[...] * CAP + slot[...], -100000).astype(F32)
    weight = jnp.where(take, gate_w[...], 0.0)
    keys = table[pl.ds(0, slots), 0:1]
    pick = jnp.where((keys == code[0:1, :]) | (keys == code[1:2, :]), 1.0, 0.0).astype(BF16)
    for h in range(CHUNKS):
        S[h] = dot(pick, tok[:, pl.ds(h * dc, dc)]).astype(BF16).reshape(X, Z * ten, dc)
    pl.semaphore_wait(barrier, len(peers))
    x_order = sorted(range(1, X), key=lambda d: -min(d, X - d))
    z_order = sorted(range(1, Z), key=lambda d: -min(d, Z - d))
    x_copies = [[push(S.at[h, xr(d)], B1.at[h, x], dev(yl, xr(d), z, yh, c)) for d in x_order] for h in range(CHUNKS)]
    for h in range(CHUNKS):
        B1[h, x] = S[h, x]

    def low(rows_):
        return lax.broadcasted_iota(jnp.int32, (rows_, 128), 1) < 64

    g_last, u_last = dg[:, pl.ds(512, 128)].astype(F32), du[:, pl.ds(512, 128)].astype(F32)
    h_last = dh[:, pl.ds(512, 128)].astype(F32)
    h_turned = pltpu.roll(h_last, 64, axis=1)
    for h in range(2):
        for j in range(2):
            Ws[h, :, pl.ds(j * 256, 128)] = dg[:, pl.ds((h * 2 + j) * 128, 128)]
            Ws[h, :, pl.ds(j * 256 + 128, 128)] = du[:, pl.ds((h * 2 + j) * 128, 128)]
        Hs[h, :, pl.ds(0, 256)] = dh[:, pl.ds(h * 256, 256)]
    Ws[0, :, pl.ds(512, 128)] = jnp.where(low(rb), g_last, pltpu.roll(u_last, 64, axis=1)).astype(BF16)
    Ws[1, :, pl.ds(512, 128)] = jnp.where(low(rb), pltpu.roll(g_last, 64, axis=1), u_last).astype(BF16)
    Hs[0, :, pl.ds(256, 128)] = jnp.where(low(n_tok), h_last, h_turned).astype(BF16)
    Hs[1, :, pl.ds(256, 128)] = jnp.where(low(n_tok), h_turned, h_last).astype(BF16)
    sw_w = push(Ws.at[1 - yl], Wd.at[yl, x, z], partner)
    sw_h = push(Hs.at[1 - yl], H.at[yl], partner)
    Wd[yl, x, z] = Ws[yl]
    H[yl] = Hs[yl]

    T[yl, :, lanes(t, dq)] = tok[...]
    t_sib = [push(tok, T.at[yl, :, lanes(t, dq)], sibling)]
    t_first = []
    for dyl, dyh in others:
        yl_, yh_ = chip(dyl, dyh)
        t_first.append(push(tok, T.at[yl, :, lanes(t, dq)], dev(yl_, x, z, yh_, c)))

    fwd_steps, bwd_steps = Z // 2, (Z - 1) // 2
    a_fwd, a_bwd, a_x, b_x, b_fwd, b_bwd = [], [], [], [], [], []
    z_next, z_prev = dev(yl, x, zr(1), yh, c), dev(yl, x, zr(-1), yh, c)

    def a_spread(zz):
        for d in x_order:
            a_x.append(push(Wd.at[0, x, zz], Wd.at[0, x, zz], dev(yl, xr(d), z, yh, c)))

    def ag_start():
        sw_w.wait_recv()
        for d in x_order:
            b_x.append(push(Wd.at[1, x, z], Wd.at[1, x, z], dev(yl, xr(d), z, yh, c)))
        a_fwd.append(push(Wd.at[0, x, z], Wd.at[0, x, z], z_next))
        if bwd_steps:
            a_bwd.append(push(Wd.at[0, x, z], Wd.at[0, x, z], z_prev))
        a_spread(z)

    def b_start():
        for copy in b_x:
            copy.wait_recv()
        b_fwd.append(push(Wd.at[1, :, z], Wd.at[1, :, z], z_next))
        if bwd_steps:
            b_bwd.append(push(Wd.at[1, :, z], Wd.at[1, :, z], z_prev))

    def a_step(s):
        def run():
            a_fwd[s - 1].wait_recv()
            zz = zr(-s)
            if s < fwd_steps:
                a_fwd.append(push(Wd.at[0, x, zz], Wd.at[0, x, zz], z_next))
            a_spread(zz)
            if s <= bwd_steps:
                a_bwd[s - 1].wait_recv()
                zz = zr(s)
                if s < bwd_steps:
                    a_bwd.append(push(Wd.at[0, x, zz], Wd.at[0, x, zz], z_prev))
                a_spread(zz)
        return run

    def b_step(s):
        def run():
            b_fwd[s - 1].wait_recv()
            if s < fwd_steps:
                zz = zr(-s)
                b_fwd.append(push(Wd.at[1, :, zz], Wd.at[1, :, zz], z_next))
            if s <= bwd_steps:
                b_bwd[s - 1].wait_recv()
                if s < bwd_steps:
                    zz = zr(s)
                    b_bwd.append(push(Wd.at[1, :, zz], Wd.at[1, :, zz], z_prev))
        return run

    ag_tasks = [ag_start, b_start]
    for s in range(1, fwd_steps + 1):
        ag_tasks += [a_step(s), b_step(s)]

    def service(place):
        for _ in range(SERVICE.get(place, 0)):
            if ag_tasks:
                ag_tasks.pop(0)()

    def build_order(k):
        across = lax.broadcasted_iota(jnp.int32, (rows, rows), 1).astype(F32)
        perms[k] = jnp.where(across == table[:, 1 + k:2 + k], 1.0, 0.0).astype(BF16)

    build_order(0)
    build_order(1)
    z_copies = []
    for h in range(CHUNKS):
        for copy in x_copies[h]:
            copy.wait_recv()
        B1p[h] = dot(perms[0], stack(B1[h].reshape(slots, dc))).astype(BF16).reshape(Z, 2 * X * ten, w)
        z_copies.append([push(B1p.at[h, zr(d)], B2.at[h, z], dev(yl, x, zr(d), yh, c)) for d in z_order])
        B2[h, z] = B1p[h, z]
        service(f"x{h}")

    for (dyl, dyh), copy in zip(others, t_first):
        copy.wait_recv()
        yl_, yh_ = chip(dyl, dyh)
        held = T.at[yl_, :, lanes(yh_ * 2 + c, dq)]
        t_sib.append(push(held, held, sibling))
    build_order(2)
    build_order(3)
    service("t")

    y_copies, y_sib = [], []
    for h in range(CHUNKS):
        for copy in z_copies[h]:
            copy.wait_recv()
        B2p[h] = spread(dot(perms[1], B2[h].reshape(rows, w))).astype(BF16).reshape(2, half, dc)
        here = Xe.at[h, yl, :, lanes(t, dc)]
        sends = []
        for dyl, dyh in others:
            yl_, yh_ = chip(dyl, dyh)
            sends.append(push(B2p.at[h, yl_], here, dev(yl_, x, z, yh_, c)))
        y_copies.append(sends)
        y_sib.append([push(B2p.at[h, yl], here, sibling)])
        Xe[h, yl, :, lanes(t, dc)] = B2p[h, yl]
        service(f"z{h}")

    for h in range(CHUNKS):
        for i in (1, 2, 0):
            y_copies[h][i].wait_recv()
            yl_, yh_ = chip(*others[i])
            held = Xe.at[h, yl_, :, lanes(yh_ * 2 + c, dc)]
            y_sib[h].append(push(held, held, sibling))
        service(f"y{h}")
        if h == 0:
            for copy in weight_loads:
                copy.wait()
        for copy in y_sib[h]:
            copy.wait_recv()
        for j in range(n_tiles):
            cols = pl.ds(j * 256, 256)
            pre = dot(Xe[h].reshape(slots, 4 * dc), Wx[:, h, :, cols].reshape(4 * dc, 256))
            if h > 0:
                pre = pre + Epre[:, cols]
            if h < CHUNKS - 1:
                Epre[:, cols] = pre
                continue
            upstream = eh[:, pl.ds(j * 128, 128)].astype(F32)
            gate_back, up_back = backs(pre[:, :128], pre[:, 128:], upstream)
            Eback[:, pl.ds(j * 256, 128)] = gate_back.astype(BF16)
            Eback[:, pl.ds(j * 256 + 128, 128)] = up_back.astype(BF16)
        service(f"f{h}")

    e_sib, e_x = {}, {}
    for h in range(CHUNKS):
        for dyh in (1, 0):
            yh_ = chip(0, dyh)[1]
            Esib_s[h, dyh] = nt(Eback[...], Wx[yh_ * 2 + 1 - c, h]).astype(BF16)
            e_sib[h, dyh] = push(Esib_s.at[h, dyh], Esib_r.at[h, dyh], sibling)
        for dyh in (1, 0):
            yh_ = chip(0, dyh)[1]
            part = nt(Eback[...], Wx[yh_ * 2 + c, h])
            e_sib[h, dyh].wait_recv()
            total = (part + Esib_r[h, dyh].astype(F32)).reshape(2, half, dc)
            Ex_s[h, dyh] = total.astype(BF16)
            for dyl in (0, 1):
                if dyl or dyh:
                    yl_ = chip(dyl, dyh)[0]
                    e_x[h, dyl, dyh] = push(Ex_s.at[h, dyh, yl_], Ex_r.at[h, dyl, dyh], dev(yl_, x, z, yh_, c))
            if not dyh:
                Etot[h] = total
        service(f"b{h}")

    def dense_forward():
        sw_h.wait_recv()
        for copy in t_sib:
            copy.wait_recv()
        while ag_tasks:
            ag_tasks.pop(0)()
        for copy in a_x:
            copy.wait_recv()
        tokens = T[...].reshape(2 * n_tok, T.shape[2])
        for j in range(2):
            pre = dot(tokens, Wd[:, :, :, :, pl.ds(j * 256, 256)].reshape(experts * rb, 256))
            upstream = H[:, :, pl.ds(j * 128, 128)].reshape(2 * n_tok, 128).astype(F32)
            gate_back, up_back = backs(pre[:, :128], pre[:, 128:], upstream)
            Dback[:, pl.ds(j * 256, 128)] = gate_back.astype(BF16)
            Dback[:, pl.ds(j * 256 + 128, 128)] = up_back.astype(BF16)
        pre = dot(tokens, Wd[:, :, :, :, pl.ds(512, 128)].reshape(experts * rb, 128))
        turned = pltpu.roll(pre, 64, axis=1)
        low_ = low(2 * n_tok)
        upstream = H[:, :, pl.ds(256, 128)].reshape(2 * n_tok, 128).astype(F32)
        gate_back, up_back = backs(jnp.where(low_, pre, turned), jnp.where(low_, turned, pre), upstream)
        Dback[:, pl.ds(512, 128)] = jnp.where(low_, gate_back, up_back).astype(BF16)

    def dense_share(t_):
        block = Wd[t_ // 2, pl.ds(lax.rem(t_, 2) * (X // 2), X // 2)]
        return nt(Dback[...], block.reshape(dq, 640))

    d_sib, d_x = {}, {}

    def dense_back():
        for dyh in (1, 0):
            yh_ = chip(0, dyh)[1]
            Dsib_s[dyh] = dense_share(yh_ * 2 + 1 - c).astype(BF16).reshape(2, n_tok, dq)
            d_sib[dyh] = push(Dsib_s.at[dyh], Dsib_r.at[dyh], sibling)
        for dyh in (1, 0):
            yh_ = chip(0, dyh)[1]
            part = dense_share(yh_ * 2 + c)
            d_sib[dyh].wait_recv()
            total = part.reshape(2, n_tok, dq) + Dsib_r[dyh].astype(F32)
            Dx_s[dyh] = total.astype(BF16)
            for dyl in (0, 1):
                if dyl or dyh:
                    yl_ = chip(dyl, dyh)[0]
                    d_x[dyl, dyh] = push(Dx_s.at[dyh, yl_], Dx_r.at[dyl, dyh], dev(yl_, x, z, yh_, c))
            if not dyh:
                Dtot[...] = total

    if DENSE == 0:
        dense_forward()
        dense_back()

    z_back = []
    for h in range(CHUNKS):
        for dyl, dyh in others:
            e_x[h, dyl, dyh].wait_recv()
        R2[h, yl] = (Etot[h, yl] + Ex_r[h, 0, 1].astype(F32)).astype(BF16)
        R2[h, 1 - yl] = (Ex_r[h, 1, 0].astype(F32) + Ex_r[h, 1, 1].astype(F32)).astype(BF16)
        Z2[h] = dot(perms[2], stack(R2[h].reshape(slots, dc))).astype(BF16).reshape(Z, 2 * X * ten, w)
        z_back.append([push(Z2.at[h, zr(d)], ZB.at[h, z], dev(yl, x, zr(d), yh, c)) for d in z_order])
        ZB[h, z] = Z2[h, z]
        if DENSE == 1 and h == 0:
            dense_forward()
    if DENSE == 1:
        dense_back()
    if DENSE == 2:
        dense_forward()
        dense_back()
    x_back = []
    for h in range(CHUNKS):
        for copy in z_back[h]:
            copy.wait_recv()
        ZBp[h] = spread(dot(perms[3], ZB[h].reshape(rows, w))).astype(BF16).reshape(X, Z * ten, dc)
        x_back.append([push(ZBp.at[h, xr(d)], XB.at[h, x], dev(yl, xr(d), z, yh, c)) for d in x_order])
        XB[h, x] = ZBp[h, x]

    for dyl, dyh in others:
        d_x[dyl, dyh].wait_recv()
    out_sum = (
        res[...].astype(F32) + Dtot[yl] + Dx_r[0, 1].astype(F32) + Dx_r[1, 0].astype(F32) + Dx_r[1, 1].astype(F32)
    )
    Dtot[0] = out_sum
    down = jnp.concatenate([code, weight, jnp.zeros((124, 128), F32)], axis=0).T
    hots = [jnp.where(key_lane[0:1, :] == down[:, k:k + 1], 1.0, 0.0).astype(BF16) for k in range(2)]
    for h in range(CHUNKS):
        for copy in x_back[h]:
            copy.wait_recv()
        returned = XB[h].reshape(slots, dc)
        total = Dtot[0, :, pl.ds(h * dc, dc)]
        for k in range(2):
            total = total + down[:, 2 + k:3 + k] * dot(hots[k], returned)
        out[:, pl.ds(h * dc, dc)] = total.astype(BF16)
    for copy in pending:
        copy.wait_send()


SERVICE = {"x1": 1, "z1": 1, "y0": 1, "f0": 1, "y1": 1, "f1": 2, "b0": 2, "b1": 1}
DENSE = 1
N_SEMS = 256


def run_kernel(tok, ids, slot, kept, gate_w, dg, du, dh, eg, eu, eh, res):
    experts, slots, ten, rows = sizes()
    half = slots // 2
    n_tok, dq = tok.shape
    d = dq * 4
    dc = dq // CHUNKS
    w = dc // 2
    rb = dg.shape[0]
    table, key_lane = tables()
    vm = pl.BlockSpec(memory_space=pltpu.VMEM)
    hbm = pl.BlockSpec(memory_space=pl.ANY)
    V = pltpu.VMEM
    C = CHUNKS
    wide = eg.shape[1] * 2
    eg, eu = (m.reshape(4, C, dc, m.shape[1]) for m in (eg, eu))
    return pl.pallas_call(
        kernel,
        out_shape=jax.ShapeDtypeStruct((n_tok, dq), BF16),
        in_specs=[vm] * 8 + [hbm, hbm] + [vm] * 4,
        out_specs=vm,
        scratch_shapes=[
            V((2, n_tok, d), BF16),
            V((2, rb, 640), BF16),
            V((2, n_tok, 384), BF16),
            V((2, n_tok, 384), BF16),
            V((2, X, Z, rb, 640), BF16),
            V((4, C, dc, wide), BF16),
            V((4, rows, rows), BF16),
            V((C, X, Z * ten, dc), BF16),
            V((C, X, Z * ten, dc), BF16),
            V((C, Z, 2 * X * ten, w), BF16),
            V((C, Z, 2 * X * ten, w), BF16),
            V((C, 2, half, dc), BF16),
            V((C, 2, half, 4 * dc), BF16),
            V((slots, wide), F32),
            V((slots, wide), BF16),
            V((C, 2, slots, dc), BF16),
            V((C, 2, slots, dc), BF16),
            V((C, 2, 2, half, dc), BF16),
            V((C, 2, 2, half, dc), BF16),
            V((C, 2, half, dc), F32),
            V((C, 2, half, dc), BF16),
            V((C, Z, 2 * X * ten, w), BF16),
            V((C, Z, 2 * X * ten, w), BF16),
            V((C, X, Z * ten, dc), BF16),
            V((C, X, Z * ten, dc), BF16),
            V((2 * n_tok, 640), BF16),
            V((2, 2, n_tok, dq), BF16),
            V((2, 2, n_tok, dq), BF16),
            V((2, 2, n_tok, dq), BF16),
            V((2, 2, n_tok, dq), BF16),
            V((2, n_tok, dq), F32),
            pltpu.SemaphoreType.DMA((N_SEMS,)),
            pltpu.SemaphoreType.DMA((N_SEMS,)),
            pltpu.SemaphoreType.DMA((16,)),
        ],
        compiler_params=pltpu.CompilerParams(
            collective_id=0, has_side_effects=True, vmem_limit_bytes=60 * 1024 * 1024
        ),
    )(
        tok, ids, slot, kept, gate_w, dg, du, dh, eg, eu, eh, res,
        jnp.asarray(table), jnp.asarray(key_lane),
    )


def body(
    tokens,
    residual_grad,
    dense_hidden,
    dense_gate,
    dense_up,
    expert_gate,
    expert_up,
    expert_hidden,
    expert_ids,
    slot_index,
    kept_mask,
    gate_weights,
):
    return run_kernel(
        tokens, expert_ids.T, slot_index.T, kept_mask.T, gate_weights.T, dense_gate, dense_up, dense_hidden,
        expert_gate[0], expert_up[0], expert_hidden[0], residual_grad,
    )


def solution(mesh):
    both = P("expert", "tensor")
    rows = P("expert", None)
    last = P("expert", None, "tensor")
    placed = (both, both, both, both, both, last, last, last, rows, rows, rows, rows)
    return jax.shard_map(body, mesh=mesh, in_specs=placed, out_specs=both, check_vma=False)
```

```python
import functools

import jax
import jax.numpy as jnp
import numpy as np
from jax import lax
from jax.experimental import pallas as pl
from jax.experimental.pallas import tpu as pltpu
from jax.sharding import PartitionSpec as P

MESH = pl.DeviceIdType.MESH
F32, BF16 = jnp.float32, jnp.bfloat16

X, Z = 4, 8
CAP = 5
CHUNKS = 4


def sizes():
    experts = 2 * X * Z
    return experts, experts * CAP, 2 * CAP, 2 * experts * CAP


def tables():
    experts, slots, ten, rows = sizes()
    keys = np.zeros((rows,), np.float32)
    first = np.zeros((rows, rows), np.float32)
    second = np.zeros((rows, rows), np.float32)
    for x in range(X):
        for z in range(Z):
            for e in range(2):
                for s in range(CAP):
                    by_xz = (x * Z + z) * ten + e * CAP + s
                    keys[by_xz] = (e * X * Z + x * Z + z) * CAP + s
                    for half in range(2):
                        by_zx = (z * 2 + half) * X * ten + x * ten + e * CAP + s
                        first[by_zx, half * slots + by_xz] = 1.0
                        second[half * slots + e * (slots // 2) + (x * Z + z) * CAP + s, by_zx] = 1.0
    columns = np.zeros((rows, 128), np.float32)
    columns[:, 0] = keys
    for k, order in enumerate((first, second, second.T, first.T)):
        columns[:, 1 + k] = np.argmax(order, axis=1)
    key_lane = np.broadcast_to(keys[None, :slots], (8, slots)).astype(np.float32)
    return columns, key_lane


def backs(gate, up, upstream):
    s = jax.nn.sigmoid(gate)
    weighted = upstream * s
    return weighted * up * (1.0 + gate * (1.0 - s)), weighted * gate


def nt(a, b):
    return lax.dot_general(a, b, (((1,), (1,)), ((), ())), preferred_element_type=F32)


def dot(a, b):
    return jnp.dot(a, b, preferred_element_type=F32)


def stack(v):
    w = v.shape[1] // 2
    return jnp.concatenate([v[:, :w], v[:, w:]], axis=0)


def spread(v):
    n = v.shape[0] // 2
    return jnp.concatenate([v[:n], v[n:]], axis=1)


def kernel(
    tok, ids, slot, kept, gate_w, dg, du, dh, eg, eu, eh, res, table, key_lane,
    out,
    T, Ws, Hs, H, Wd, Wx, perms, S, B1, B1p, B2, B2p, Xe, Epre, Eback, Esib_s, Esib_r, Ex_s, Ex_r, Etot, R2,
    Z2, ZB, ZBp, XB, Dback, Dsib_s, Dsib_r, Dx_s, Dx_r, Dtot,
    send, recv, local,
):
    experts, slots, ten, rows = sizes()
    half = slots // 2
    n_tok, dq = tok.shape
    dc = dq // CHUNKS
    w = dc // 2
    rb = dg.shape[0]
    e = lax.axis_index("expert")
    t = lax.axis_index("tensor")
    yl, x, z = e // (X * Z), lax.rem(e // Z, X), lax.rem(e, Z)
    yh, c = t // 2, lax.rem(t, 2)

    def dev(yl_, x_, z_, yh_, c_):
        return (yl_ * (X * Z) + x_ * Z + z_, yh_ * 2 + c_)

    def lanes(t_, width):
        return pl.ds(pl.multiple_of(t_ * width, width), width)

    def xr(d):
        return lax.rem(x + d, X)

    def zr(d):
        return lax.rem(z + d + Z, Z)

    partner = dev(1 - yl, x, z, yh, c)
    sibling = dev(yl, x, z, yh, 1 - c)
    others = [(0, 1), (1, 0), (1, 1)]

    def chip(dyl, dyh):
        return (1 - yl if dyl else yl), (1 - yh if dyh else yh)

    pending = []

    def push(src, dst, device):
        i = len(pending)
        copy = pltpu.make_async_remote_copy(
            src_ref=src, dst_ref=dst, send_sem=send.at[i], recv_sem=recv.at[i],
            device_id=device, device_id_type=MESH,
        )
        copy.start()
        pending.append(copy)
        return copy

    locals_ = []

    def load(src, dst):
        copy = pltpu.make_async_copy(src, dst, local.at[len(locals_)])
        copy.start()
        locals_.append(copy)
        return copy

    barrier = pltpu.get_barrier_semaphore()
    peers = [dev(yl, xr(d), z, yh, c) for d in range(1, X)]
    peers += [dev(yl, x, zr(d), yh, c) for d in range(1, Z)]
    for dyl, dyh in others:
        yl_, yh_ = chip(dyl, dyh)
        peers += [dev(yl_, x, z, yh_, c)]
    peers += [sibling]
    for peer in peers:
        pl.semaphore_signal(barrier, inc=1, device_id=peer, device_id_type=MESH)

    weight_loads = []
    n_tiles = eg.shape[3] // 128
    for j in range(n_tiles):
        weight_loads.append(load(eg.at[:, :, :, pl.ds(j * 128, 128)], Wx.at[:, :, :, pl.ds(j * 256, 128)]))
        weight_loads.append(load(eu.at[:, :, :, pl.ds(j * 128, 128)], Wx.at[:, :, :, pl.ds(j * 256 + 128, 128)]))

    take = (kept[...] == 1) & (slot[...] < CAP)
    code = jnp.where(take, ids[...] * CAP + slot[...], -100000).astype(F32)
    weight = jnp.where(take, gate_w[...], 0.0)
    keys = table[pl.ds(0, slots), 0:1]
    pick = jnp.where((keys == code[0:1, :]) | (keys == code[1:2, :]), 1.0, 0.0).astype(BF16)
    for h in range(CHUNKS):
        S[h] = dot(pick, tok[:, pl.ds(h * dc, dc)]).astype(BF16).reshape(X, Z * ten, dc)
    pl.semaphore_wait(barrier, len(peers))
    x_order = sorted(range(1, X), key=lambda d: -min(d, X - d))
    z_order = sorted(range(1, Z), key=lambda d: -min(d, Z - d))
    x_copies = [[push(S.at[h, xr(d)], B1.at[h, x], dev(yl, xr(d), z, yh, c)) for d in x_order] for h in range(CHUNKS)]
    for h in range(CHUNKS):
        B1[h, x] = S[h, x]

    def low(rows_):
        return lax.broadcasted_iota(jnp.int32, (rows_, 128), 1) < 64

    g_last, u_last = dg[:, pl.ds(512, 128)].astype(F32), du[:, pl.ds(512, 128)].astype(F32)
    h_last = dh[:, pl.ds(512, 128)].astype(F32)
    h_turned = pltpu.roll(h_last, 64, axis=1)
    for h in range(2):
        for j in range(2):
            Ws[h, :, pl.ds(j * 256, 128)] = dg[:, pl.ds((h * 2 + j) * 128, 128)]
            Ws[h, :, pl.ds(j * 256 + 128, 128)] = du[:, pl.ds((h * 2 + j) * 128, 128)]
        Hs[h, :, pl.ds(0, 256)] = dh[:, pl.ds(h * 256, 256)]
    Ws[0, :, pl.ds(512, 128)] = jnp.where(low(rb), g_last, pltpu.roll(u_last, 64, axis=1)).astype(BF16)
    Ws[1, :, pl.ds(512, 128)] = jnp.where(low(rb), pltpu.roll(g_last, 64, axis=1), u_last).astype(BF16)
    Hs[0, :, pl.ds(256, 128)] = jnp.where(low(n_tok), h_last, h_turned).astype(BF16)
    Hs[1, :, pl.ds(256, 128)] = jnp.where(low(n_tok), h_turned, h_last).astype(BF16)
    sw_w = push(Ws.at[1 - yl], Wd.at[yl, x, z], partner)
    sw_h = push(Hs.at[1 - yl], H.at[yl], partner)
    Wd[yl, x, z] = Ws[yl]
    H[yl] = Hs[yl]

    T[yl, :, lanes(t, dq)] = tok[...]
    t_sib = [push(tok, T.at[yl, :, lanes(t, dq)], sibling)]
    t_first = []
    for dyl, dyh in others:
        yl_, yh_ = chip(dyl, dyh)
        t_first.append(push(tok, T.at[yl, :, lanes(t, dq)], dev(yl_, x, z, yh_, c)))

    fwd_steps, bwd_steps = Z // 2, (Z - 1) // 2
    a_fwd, a_bwd, a_x, b_x, b_fwd, b_bwd = [], [], [], [], [], []
    z_next, z_prev = dev(yl, x, zr(1), yh, c), dev(yl, x, zr(-1), yh, c)

    def a_spread(zz):
        for d in x_order:
            a_x.append(push(Wd.at[0, x, zz], Wd.at[0, x, zz], dev(yl, xr(d), z, yh, c)))

    def ag_start():
        sw_w.wait_recv()
        for d in x_order:
            b_x.append(push(Wd.at[1, x, z], Wd.at[1, x, z], dev(yl, xr(d), z, yh, c)))
        a_fwd.append(push(Wd.at[0, x, z], Wd.at[0, x, z], z_next))
        if bwd_steps:
            a_bwd.append(push(Wd.at[0, x, z], Wd.at[0, x, z], z_prev))
        a_spread(z)

    def b_start():
        for copy in b_x:
            copy.wait_recv()
        b_fwd.append(push(Wd.at[1, :, z], Wd.at[1, :, z], z_next))
        if bwd_steps:
            b_bwd.append(push(Wd.at[1, :, z], Wd.at[1, :, z], z_prev))

    def a_step(s):
        def run():
            a_fwd[s - 1].wait_recv()
            zz = zr(-s)
            if s < fwd_steps:
                a_fwd.append(push(Wd.at[0, x, zz], Wd.at[0, x, zz], z_next))
            a_spread(zz)
            if s <= bwd_steps:
                a_bwd[s - 1].wait_recv()
                zz = zr(s)
                if s < bwd_steps:
                    a_bwd.append(push(Wd.at[0, x, zz], Wd.at[0, x, zz], z_prev))
                a_spread(zz)
        return run

    def b_step(s):
        def run():
            b_fwd[s - 1].wait_recv()
            if s < fwd_steps:
                zz = zr(-s)
                some = pl.ds(0, X // 2 if s == bwd_steps else X)
                b_fwd.append(push(Wd.at[1, some, zz], Wd.at[1, some, zz], z_next))
            if len(b_bwd) >= s:
                b_bwd[s - 1].wait_recv()
            if s < fwd_steps:
                zz = zr(s)
                some = pl.ds(X // 2, X - X // 2) if s == bwd_steps else pl.ds(0, X)
                b_bwd.append(push(Wd.at[1, some, zz], Wd.at[1, some, zz], z_prev))
        return run

    ag_tasks = [ag_start, b_start]
    for s in range(1, fwd_steps + 1):
        ag_tasks += [a_step(s), b_step(s)]

    def service(place):
        for _ in range(SERVICE.get(place, 0)):
            if ag_tasks:
                ag_tasks.pop(0)()

    def build_order(k):
        across = lax.broadcasted_iota(jnp.int32, (rows, rows), 1).astype(F32)
        perms[k] = jnp.where(across == table[:, 1 + k:2 + k], 1.0, 0.0).astype(BF16)

    build_order(0)
    build_order(1)
    z_copies = []
    for h in range(CHUNKS):
        for copy in x_copies[h]:
            copy.wait_recv()
        B1p[h] = dot(perms[0], stack(B1[h].reshape(slots, dc))).astype(BF16).reshape(Z, 2 * X * ten, w)
        z_copies.append([push(B1p.at[h, zr(d)], B2.at[h, z], dev(yl, x, zr(d), yh, c)) for d in z_order])
        B2[h, z] = B1p[h, z]
        service(f"x{h}")

    for (dyl, dyh), copy in zip(others, t_first):
        copy.wait_recv()
        yl_, yh_ = chip(dyl, dyh)
        held = T.at[yl_, :, lanes(yh_ * 2 + c, dq)]
        t_sib.append(push(held, held, sibling))
    build_order(2)
    build_order(3)
    service("t")

    y_copies, y_sib = [], []
    for h in range(CHUNKS):
        for copy in z_copies[h]:
            copy.wait_recv()
        B2p[h] = spread(dot(perms[1], B2[h].reshape(rows, w))).astype(BF16).reshape(2, half, dc)
        here = Xe.at[h, yl, :, lanes(t, dc)]
        sends = []
        for dyl, dyh in others:
            yl_, yh_ = chip(dyl, dyh)
            sends.append(push(B2p.at[h, yl_], here, dev(yl_, x, z, yh_, c)))
        y_copies.append(sends)
        y_sib.append([push(B2p.at[h, yl], here, sibling)])
        Xe[h, yl, :, lanes(t, dc)] = B2p[h, yl]
        service(f"z{h}")

    for h in range(CHUNKS):
        for i in (1, 2, 0):
            y_copies[h][i].wait_recv()
            yl_, yh_ = chip(*others[i])
            held = Xe.at[h, yl_, :, lanes(yh_ * 2 + c, dc)]
            y_sib[h].append(push(held, held, sibling))
        service(f"y{h}")
        if h == 0:
            for copy in weight_loads:
                copy.wait()
        for copy in y_sib[h]:
            copy.wait_recv()
        for j in range(n_tiles):
            cols = pl.ds(j * 256, 256)
            pre = dot(Xe[h].reshape(slots, 4 * dc), Wx[:, h, :, cols].reshape(4 * dc, 256))
            if h > 0:
                pre = pre + Epre[:, cols]
            if h < CHUNKS - 1:
                Epre[:, cols] = pre
                continue
            upstream = eh[:, pl.ds(j * 128, 128)].astype(F32)
            gate_back, up_back = backs(pre[:, :128], pre[:, 128:], upstream)
            Eback[:, pl.ds(j * 256, 128)] = gate_back.astype(BF16)
            Eback[:, pl.ds(j * 256 + 128, 128)] = up_back.astype(BF16)
        service(f"f{h}")

    e_sib, e_x = {}, {}
    for h in range(CHUNKS):
        for dyh in (1, 0):
            yh_ = chip(0, dyh)[1]
            Esib_s[h, dyh] = nt(Eback[...], Wx[yh_ * 2 + 1 - c, h]).astype(BF16)
            e_sib[h, dyh] = push(Esib_s.at[h, dyh], Esib_r.at[h, dyh], sibling)
        for dyh in (1, 0):
            yh_ = chip(0, dyh)[1]
            part = nt(Eback[...], Wx[yh_ * 2 + c, h])
            e_sib[h, dyh].wait_recv()
            total = (part + Esib_r[h, dyh].astype(F32)).reshape(2, half, dc)
            Ex_s[h, dyh] = total.astype(BF16)
            for dyl in (0, 1):
                if dyl or dyh:
                    yl_ = chip(dyl, dyh)[0]
                    e_x[h, dyl, dyh] = push(Ex_s.at[h, dyh, yl_], Ex_r.at[h, dyl, dyh], dev(yl_, x, z, yh_, c))
            if not dyh:
                Etot[h] = total
        service(f"b{h}")

    def dense_forward():
        sw_h.wait_recv()
        for copy in t_sib:
            copy.wait_recv()
        while ag_tasks:
            ag_tasks.pop(0)()
        for copy in a_x:
            copy.wait_recv()
        tokens = T[...].reshape(2 * n_tok, T.shape[2])
        for j in range(2):
            pre = dot(tokens, Wd[:, :, :, :, pl.ds(j * 256, 256)].reshape(experts * rb, 256))
            upstream = H[:, :, pl.ds(j * 128, 128)].reshape(2 * n_tok, 128).astype(F32)
            gate_back, up_back = backs(pre[:, :128], pre[:, 128:], upstream)
            Dback[:, pl.ds(j * 256, 128)] = gate_back.astype(BF16)
            Dback[:, pl.ds(j * 256 + 128, 128)] = up_back.astype(BF16)
        pre = dot(tokens, Wd[:, :, :, :, pl.ds(512, 128)].reshape(experts * rb, 128))
        turned = pltpu.roll(pre, 64, axis=1)
        low_ = low(2 * n_tok)
        upstream = H[:, :, pl.ds(256, 128)].reshape(2 * n_tok, 128).astype(F32)
        gate_back, up_back = backs(jnp.where(low_, pre, turned), jnp.where(low_, turned, pre), upstream)
        Dback[:, pl.ds(512, 128)] = jnp.where(low_, gate_back, up_back).astype(BF16)

    def dense_share(t_):
        block = Wd[t_ // 2, pl.ds(lax.rem(t_, 2) * (X // 2), X // 2)]
        return nt(Dback[...], block.reshape(dq, 640))

    d_sib, d_x = {}, {}

    def dense_back():
        for dyh in (1, 0):
            yh_ = chip(0, dyh)[1]
            Dsib_s[dyh] = dense_share(yh_ * 2 + 1 - c).astype(BF16).reshape(2, n_tok, dq)
            d_sib[dyh] = push(Dsib_s.at[dyh], Dsib_r.at[dyh], sibling)
        for dyh in (1, 0):
            yh_ = chip(0, dyh)[1]
            part = dense_share(yh_ * 2 + c)
            d_sib[dyh].wait_recv()
            total = part.reshape(2, n_tok, dq) + Dsib_r[dyh].astype(F32)
            Dx_s[dyh] = total.astype(BF16)
            for dyl in (0, 1):
                if dyl or dyh:
                    yl_ = chip(dyl, dyh)[0]
                    d_x[dyl, dyh] = push(Dx_s.at[dyh, yl_], Dx_r.at[dyl, dyh], dev(yl_, x, z, yh_, c))
            if not dyh:
                Dtot[...] = total

    z_back = []
    for h in range(CHUNKS):
        for dyl, dyh in others:
            e_x[h, dyl, dyh].wait_recv()
        R2[h, yl] = (Etot[h, yl] + Ex_r[h, 0, 1].astype(F32)).astype(BF16)
        R2[h, 1 - yl] = (Ex_r[h, 1, 0].astype(F32) + Ex_r[h, 1, 1].astype(F32)).astype(BF16)
        Z2[h] = dot(perms[2], stack(R2[h].reshape(slots, dc))).astype(BF16).reshape(Z, 2 * X * ten, w)
        z_back.append([push(Z2.at[h, zr(d)], ZB.at[h, z], dev(yl, x, zr(d), yh, c)) for d in z_order])
        ZB[h, z] = Z2[h, z]
        if h == CHUNKS // 2 - 1:
            dense_forward()
            dense_back()
    x_back = []
    for h in range(CHUNKS):
        for copy in z_back[h]:
            copy.wait_recv()
        ZBp[h] = spread(dot(perms[3], ZB[h].reshape(rows, w))).astype(BF16).reshape(X, Z * ten, dc)
        x_back.append([push(ZBp.at[h, xr(d)], XB.at[h, x], dev(yl, xr(d), z, yh, c)) for d in x_order])
        XB[h, x] = ZBp[h, x]

    for dyl, dyh in others:
        d_x[dyl, dyh].wait_recv()
    out_sum = (
        res[...].astype(F32) + Dtot[yl] + Dx_r[0, 1].astype(F32) + Dx_r[1, 0].astype(F32) + Dx_r[1, 1].astype(F32)
    )
    Dtot[0] = out_sum
    down = jnp.concatenate([code, weight, jnp.zeros((124, 128), F32)], axis=0).T
    hots = [jnp.where(key_lane[0:1, :] == down[:, k:k + 1], 1.0, 0.0).astype(BF16) for k in range(2)]
    for h in range(CHUNKS):
        for copy in x_back[h]:
            copy.wait_recv()
        returned = XB[h].reshape(slots, dc)
        total = Dtot[0, :, pl.ds(h * dc, dc)]
        for k in range(2):
            total = total + down[:, 2 + k:3 + k] * dot(hots[k], returned)
        out[:, pl.ds(h * dc, dc)] = total.astype(BF16)
    for copy in pending:
        copy.wait_send()


SERVICE = {"x3": 1, "t": 1, "z0": 1, "z3": 1, "y0": 1, "f2": 1, "y3": 1, "f3": 2, "b1": 1}
N_SEMS = 256


def run_kernel(tok, ids, slot, kept, gate_w, dg, du, dh, eg, eu, eh, res):
    experts, slots, ten, rows = sizes()
    half = slots // 2
    n_tok, dq = tok.shape
    d = dq * 4
    dc = dq // CHUNKS
    w = dc // 2
    rb = dg.shape[0]
    table, key_lane = tables()
    vm = pl.BlockSpec(memory_space=pltpu.VMEM)
    hbm = pl.BlockSpec(memory_space=pl.ANY)
    V = pltpu.VMEM
    C = CHUNKS
    wide = eg.shape[1] * 2
    eg, eu = (m.reshape(4, C, dc, m.shape[1]) for m in (eg, eu))
    return pl.pallas_call(
        kernel,
        out_shape=jax.ShapeDtypeStruct((n_tok, dq), BF16),
        in_specs=[vm] * 8 + [hbm, hbm] + [vm] * 4,
        out_specs=vm,
        scratch_shapes=[
            V((2, n_tok, d), BF16),
            V((2, rb, 640), BF16),
            V((2, n_tok, 384), BF16),
            V((2, n_tok, 384), BF16),
            V((2, X, Z, rb, 640), BF16),
            V((4, C, dc, wide), BF16),
            V((4, rows, rows), BF16),
            V((C, X, Z * ten, dc), BF16),
            V((C, X, Z * ten, dc), BF16),
            V((C, Z, 2 * X * ten, w), BF16),
            V((C, Z, 2 * X * ten, w), BF16),
            V((C, 2, half, dc), BF16),
            V((C, 2, half, 4 * dc), BF16),
            V((slots, wide), F32),
            V((slots, wide), BF16),
            V((C, 2, slots, dc), BF16),
            V((C, 2, slots, dc), BF16),
            V((C, 2, 2, half, dc), BF16),
            V((C, 2, 2, half, dc), BF16),
            V((C, 2, half, dc), F32),
            V((C, 2, half, dc), BF16),
            V((C, Z, 2 * X * ten, w), BF16),
            V((C, Z, 2 * X * ten, w), BF16),
            V((C, X, Z * ten, dc), BF16),
            V((C, X, Z * ten, dc), BF16),
            V((2 * n_tok, 640), BF16),
            V((2, 2, n_tok, dq), BF16),
            V((2, 2, n_tok, dq), BF16),
            V((2, 2, n_tok, dq), BF16),
            V((2, 2, n_tok, dq), BF16),
            V((2, n_tok, dq), F32),
            pltpu.SemaphoreType.DMA((N_SEMS,)),
            pltpu.SemaphoreType.DMA((N_SEMS,)),
            pltpu.SemaphoreType.DMA((16,)),
        ],
        compiler_params=pltpu.CompilerParams(
            collective_id=0, has_side_effects=True, vmem_limit_bytes=60 * 1024 * 1024
        ),
    )(
        tok, ids, slot, kept, gate_w, dg, du, dh, eg, eu, eh, res,
        jnp.asarray(table), jnp.asarray(key_lane),
    )


def body(
    tokens,
    residual_grad,
    dense_hidden,
    dense_gate,
    dense_up,
    expert_gate,
    expert_up,
    expert_hidden,
    expert_ids,
    slot_index,
    kept_mask,
    gate_weights,
):
    return run_kernel(
        tokens, expert_ids.T, slot_index.T, kept_mask.T, gate_weights.T, dense_gate, dense_up, dense_hidden,
        expert_gate[0], expert_up[0], expert_hidden[0], residual_grad,
    )


def solution(mesh):
    both = P("expert", "tensor")
    rows = P("expert", None)
    last = P("expert", None, "tensor")
    placed = (both, both, both, both, both, last, last, last, rows, rows, rows, rows)
    return jax.shard_map(body, mesh=mesh, in_specs=placed, out_specs=both, check_vma=False)
```

```python
import functools

import jax
import jax.numpy as jnp
import numpy as np
from jax import lax
from jax.experimental import pallas as pl
from jax.experimental.pallas import tpu as pltpu
from jax.sharding import PartitionSpec as P

MESH = pl.DeviceIdType.MESH
F32, BF16 = jnp.float32, jnp.bfloat16

X, Z = 4, 8
CAP = 5
CHUNKS = 4


def sizes():
    experts = 2 * X * Z
    return experts, experts * CAP, 2 * CAP, 2 * experts * CAP


def tables():
    experts, slots, ten, rows = sizes()
    keys = np.zeros((rows,), np.float32)
    first = np.zeros((rows, rows), np.float32)
    second = np.zeros((rows, rows), np.float32)
    for x in range(X):
        for z in range(Z):
            for e in range(2):
                for s in range(CAP):
                    by_xz = (x * Z + z) * ten + e * CAP + s
                    keys[by_xz] = (e * X * Z + x * Z + z) * CAP + s
                    for half in range(2):
                        by_zx = (z * 2 + half) * X * ten + x * ten + e * CAP + s
                        first[by_zx, half * slots + by_xz] = 1.0
                        second[half * slots + e * (slots // 2) + (x * Z + z) * CAP + s, by_zx] = 1.0
    columns = np.zeros((rows, 128), np.float32)
    columns[:, 0] = keys
    for k, order in enumerate((first, second, second.T, first.T)):
        columns[:, 1 + k] = np.argmax(order, axis=1)
    key_lane = np.broadcast_to(keys[None, :slots], (8, slots)).astype(np.float32)
    return columns, key_lane


def backs(gate, up, upstream):
    s = jax.nn.sigmoid(gate)
    weighted = upstream * s
    return weighted * up * (1.0 + gate * (1.0 - s)), weighted * gate


def nt(a, b):
    return lax.dot_general(a, b, (((1,), (1,)), ((), ())), preferred_element_type=F32)


def dot(a, b):
    return jnp.dot(a, b, preferred_element_type=F32)


def stack(v):
    w = v.shape[1] // 2
    return jnp.concatenate([v[:, :w], v[:, w:]], axis=0)


def spread(v):
    n = v.shape[0] // 2
    return jnp.concatenate([v[:n], v[n:]], axis=1)


def kernel(
    tok, ids, slot, kept, gate_w, dg, du, dh, eg, eu, eh, res, table, key_lane,
    out,
    T, Ws, Hs, H, Wd, Wx, perms, S, B1, B1p, B2, B2p, Xe, Epre, Eback, Esib_s, Esib_r, Ex_s, Ex_r, Etot, R2,
    Z2, ZB, ZBp, XB, Dback, Dsib_s, Dsib_r, Dx_s, Dx_r, Dtot,
    send, recv, local,
):
    experts, slots, ten, rows = sizes()
    half = slots // 2
    n_tok, dq = tok.shape
    dc = dq // CHUNKS
    w = dc // 2
    rb = dg.shape[0]
    e = lax.axis_index("expert")
    t = lax.axis_index("tensor")
    yl, x, z = e // (X * Z), lax.rem(e // Z, X), lax.rem(e, Z)
    yh, c = t // 2, lax.rem(t, 2)

    def dev(yl_, x_, z_, yh_, c_):
        return (yl_ * (X * Z) + x_ * Z + z_, yh_ * 2 + c_)

    def lanes(t_, width):
        return pl.ds(pl.multiple_of(t_ * width, width), width)

    def xr(d):
        return lax.rem(x + d, X)

    def zr(d):
        return lax.rem(z + d + Z, Z)

    partner = dev(1 - yl, x, z, yh, c)
    sibling = dev(yl, x, z, yh, 1 - c)
    others = [(0, 1), (1, 0), (1, 1)]

    def chip(dyl, dyh):
        return (1 - yl if dyl else yl), (1 - yh if dyh else yh)

    pending = []

    def push(src, dst, device):
        i = len(pending)
        copy = pltpu.make_async_remote_copy(
            src_ref=src, dst_ref=dst, send_sem=send.at[i], recv_sem=recv.at[i],
            device_id=device, device_id_type=MESH,
        )
        copy.start()
        pending.append(copy)
        return copy

    locals_ = []

    def load(src, dst):
        copy = pltpu.make_async_copy(src, dst, local.at[len(locals_)])
        copy.start()
        locals_.append(copy)
        return copy

    barrier = pltpu.get_barrier_semaphore()
    peers = [dev(yl, xr(d), z, yh, c) for d in range(1, X)]
    peers += [dev(yl, x, zr(d), yh, c) for d in range(1, Z)]
    for dyl, dyh in others:
        yl_, yh_ = chip(dyl, dyh)
        peers += [dev(yl_, x, z, yh_, c)]
    peers += [sibling]
    for peer in peers:
        pl.semaphore_signal(barrier, inc=1, device_id=peer, device_id_type=MESH)

    weight_loads = []
    n_tiles = eg.shape[3] // 128
    for j in range(n_tiles):
        weight_loads.append(load(eg.at[:, :, :, pl.ds(j * 128, 128)], Wx.at[:, :, :, pl.ds(j * 256, 128)]))
        weight_loads.append(load(eu.at[:, :, :, pl.ds(j * 128, 128)], Wx.at[:, :, :, pl.ds(j * 256 + 128, 128)]))

    take = (kept[...] == 1) & (slot[...] < CAP)
    code = jnp.where(take, ids[...] * CAP + slot[...], -100000).astype(F32)
    weight = jnp.where(take, gate_w[...], 0.0)
    keys = table[pl.ds(0, slots), 0:1]
    pick = jnp.where((keys == code[0:1, :]) | (keys == code[1:2, :]), 1.0, 0.0).astype(BF16)
    for h in range(CHUNKS):
        S[h] = dot(pick, tok[:, pl.ds(h * dc, dc)]).astype(BF16).reshape(X, Z * ten, dc)
    pl.semaphore_wait(barrier, len(peers))
    x_order = sorted(range(1, X), key=lambda d: -min(d, X - d))
    z_order = sorted(range(1, Z), key=lambda d: -min(d, Z - d))
    x_copies = [[push(S.at[h, xr(d)], B1.at[h, x], dev(yl, xr(d), z, yh, c)) for d in x_order] for h in range(CHUNKS)]
    for h in range(CHUNKS):
        B1[h, x] = S[h, x]

    def low(rows_):
        return lax.broadcasted_iota(jnp.int32, (rows_, 128), 1) < 64

    g_last, u_last = dg[:, pl.ds(512, 128)].astype(F32), du[:, pl.ds(512, 128)].astype(F32)
    h_last = dh[:, pl.ds(512, 128)].astype(F32)
    h_turned = pltpu.roll(h_last, 64, axis=1)
    for h in range(2):
        for j in range(2):
            Ws[h, :, pl.ds(j * 256, 128)] = dg[:, pl.ds((h * 2 + j) * 128, 128)]
            Ws[h, :, pl.ds(j * 256 + 128, 128)] = du[:, pl.ds((h * 2 + j) * 128, 128)]
        Hs[h, :, pl.ds(0, 256)] = dh[:, pl.ds(h * 256, 256)]
    Ws[0, :, pl.ds(512, 128)] = jnp.where(low(rb), g_last, pltpu.roll(u_last, 64, axis=1)).astype(BF16)
    Ws[1, :, pl.ds(512, 128)] = jnp.where(low(rb), pltpu.roll(g_last, 64, axis=1), u_last).astype(BF16)
    Hs[0, :, pl.ds(256, 128)] = jnp.where(low(n_tok), h_last, h_turned).astype(BF16)
    Hs[1, :, pl.ds(256, 128)] = jnp.where(low(n_tok), h_turned, h_last).astype(BF16)
    sw_w = push(Ws.at[1 - yl], Wd.at[yl, x, z], partner)
    sw_h = push(Hs.at[1 - yl], H.at[yl], partner)
    Wd[yl, x, z] = Ws[yl]
    H[yl] = Hs[yl]

    T[yl, :, lanes(t, dq)] = tok[...]
    t_sib = [push(tok, T.at[yl, :, lanes(t, dq)], sibling)]
    t_first = []
    for dyl, dyh in others:
        yl_, yh_ = chip(dyl, dyh)
        t_first.append(push(tok, T.at[yl, :, lanes(t, dq)], dev(yl_, x, z, yh_, c)))

    fwd_steps, bwd_steps = Z // 2, (Z - 1) // 2
    a_fwd, a_bwd, a_x, b_x, b_fwd, b_bwd = [], [], [], [], [], []
    z_next, z_prev = dev(yl, x, zr(1), yh, c), dev(yl, x, zr(-1), yh, c)

    def a_spread(zz):
        for d in x_order:
            a_x.append(push(Wd.at[0, x, zz], Wd.at[0, x, zz], dev(yl, xr(d), z, yh, c)))

    def ag_start():
        sw_w.wait_recv()
        for d in x_order:
            b_x.append(push(Wd.at[1, x, z], Wd.at[1, x, z], dev(yl, xr(d), z, yh, c)))
        a_fwd.append(push(Wd.at[0, x, z], Wd.at[0, x, z], z_next))
        if bwd_steps:
            a_bwd.append(push(Wd.at[0, x, z], Wd.at[0, x, z], z_prev))

    def b_start():
        for copy in b_x:
            copy.wait_recv()
        b_fwd.append(push(Wd.at[1, :, z], Wd.at[1, :, z], z_next))
        if bwd_steps:
            b_bwd.append(push(Wd.at[1, :, z], Wd.at[1, :, z], z_prev))
        a_spread(z)

    def a_step(s):
        def run():
            a_fwd[s - 1].wait_recv()
            zz = zr(-s)
            if s < fwd_steps:
                a_fwd.append(push(Wd.at[0, x, zz], Wd.at[0, x, zz], z_next))
            a_spread(zz)
            if s <= bwd_steps:
                a_bwd[s - 1].wait_recv()
                zz = zr(s)
                if s < bwd_steps:
                    a_bwd.append(push(Wd.at[0, x, zz], Wd.at[0, x, zz], z_prev))
                a_spread(zz)
        return run

    def b_step(s):
        def run():
            b_fwd[s - 1].wait_recv()
            if s < fwd_steps:
                zz = zr(-s)
                some = pl.ds(0, X // 2 if s == bwd_steps else X)
                b_fwd.append(push(Wd.at[1, some, zz], Wd.at[1, some, zz], z_next))
            if len(b_bwd) >= s:
                b_bwd[s - 1].wait_recv()
            if s < fwd_steps:
                zz = zr(s)
                some = pl.ds(X // 2, X - X // 2) if s == bwd_steps else pl.ds(0, X)
                b_bwd.append(push(Wd.at[1, some, zz], Wd.at[1, some, zz], z_prev))
        return run

    ag_tasks = [ag_start, b_start]
    for s in range(1, fwd_steps + 1):
        ag_tasks += [a_step(s), b_step(s)]

    def service(place):
        for _ in range(SERVICE.get(place, 0)):
            if ag_tasks:
                ag_tasks.pop(0)()

    def build_order(k):
        across = lax.broadcasted_iota(jnp.int32, (rows, rows), 1).astype(F32)
        perms[k] = jnp.where(across == table[:, 1 + k:2 + k], 1.0, 0.0).astype(BF16)

    build_order(0)
    build_order(1)
    z_copies = []
    for h in range(CHUNKS):
        for copy in x_copies[h]:
            copy.wait_recv()
        B1p[h] = dot(perms[0], stack(B1[h].reshape(slots, dc))).astype(BF16).reshape(Z, 2 * X * ten, w)
        z_copies.append([push(B1p.at[h, zr(d)], B2.at[h, z], dev(yl, x, zr(d), yh, c)) for d in z_order])
        B2[h, z] = B1p[h, z]
        service(f"x{h}")

    build_order(2)
    build_order(3)
    service("t")

    y_copies, y_sib = [], []
    for h in range(CHUNKS):
        for copy in z_copies[h]:
            copy.wait_recv()
        B2p[h] = spread(dot(perms[1], B2[h].reshape(rows, w))).astype(BF16).reshape(2, half, dc)
        here = Xe.at[h, yl, :, lanes(t, dc)]
        sends = []
        for dyl, dyh in others:
            yl_, yh_ = chip(dyl, dyh)
            sends.append(push(B2p.at[h, yl_], here, dev(yl_, x, z, yh_, c)))
        y_copies.append(sends)
        y_sib.append([push(B2p.at[h, yl], here, sibling)])
        Xe[h, yl, :, lanes(t, dc)] = B2p[h, yl]
        service(f"z{h}")

    for (dyl, dyh), copy in zip(others, t_first):
        copy.wait_recv()
        yl_, yh_ = chip(dyl, dyh)
        held = T.at[yl_, :, lanes(yh_ * 2 + c, dq)]
        t_sib.append(push(held, held, sibling))

    for h in range(CHUNKS):
        for i in (1, 2, 0):
            y_copies[h][i].wait_recv()
            yl_, yh_ = chip(*others[i])
            held = Xe.at[h, yl_, :, lanes(yh_ * 2 + c, dc)]
            y_sib[h].append(push(held, held, sibling))
        service(f"y{h}")
        if h == 0:
            for copy in weight_loads:
                copy.wait()
        for copy in y_sib[h]:
            copy.wait_recv()
        for j in range(n_tiles):
            cols = pl.ds(j * 256, 256)
            pre = dot(Xe[h].reshape(slots, 4 * dc), Wx[:, h, :, cols].reshape(4 * dc, 256))
            if h > 0:
                pre = pre + Epre[:, cols]
            if h < CHUNKS - 1:
                Epre[:, cols] = pre
                continue
            upstream = eh[:, pl.ds(j * 128, 128)].astype(F32)
            gate_back, up_back = backs(pre[:, :128], pre[:, 128:], upstream)
            Eback[:, pl.ds(j * 256, 128)] = gate_back.astype(BF16)
            Eback[:, pl.ds(j * 256 + 128, 128)] = up_back.astype(BF16)
        service(f"f{h}")

    e_sib, e_x = {}, {}
    for h in range(CHUNKS):
        for dyh in (1, 0):
            yh_ = chip(0, dyh)[1]
            Esib_s[h, dyh] = nt(Eback[...], Wx[yh_ * 2 + 1 - c, h]).astype(BF16)
            e_sib[h, dyh] = push(Esib_s.at[h, dyh], Esib_r.at[h, dyh], sibling)
        for dyh in (1, 0):
            yh_ = chip(0, dyh)[1]
            part = nt(Eback[...], Wx[yh_ * 2 + c, h])
            e_sib[h, dyh].wait_recv()
            total = (part + Esib_r[h, dyh].astype(F32)).reshape(2, half, dc)
            Ex_s[h, dyh] = total.astype(BF16)
            for dyl in (0, 1):
                if dyl or dyh:
                    yl_ = chip(dyl, dyh)[0]
                    e_x[h, dyl, dyh] = push(Ex_s.at[h, dyh, yl_], Ex_r.at[h, dyl, dyh], dev(yl_, x, z, yh_, c))
            if not dyh:
                Etot[h] = total
        service(f"b{h}")

    def dense_forward():
        sw_h.wait_recv()
        for copy in t_sib:
            copy.wait_recv()
        while ag_tasks:
            ag_tasks.pop(0)()
        for copy in a_x:
            copy.wait_recv()
        tokens = T[...].reshape(2 * n_tok, T.shape[2])
        for j in range(2):
            pre = dot(tokens, Wd[:, :, :, :, pl.ds(j * 256, 256)].reshape(experts * rb, 256))
            upstream = H[:, :, pl.ds(j * 128, 128)].reshape(2 * n_tok, 128).astype(F32)
            gate_back, up_back = backs(pre[:, :128], pre[:, 128:], upstream)
            Dback[:, pl.ds(j * 256, 128)] = gate_back.astype(BF16)
            Dback[:, pl.ds(j * 256 + 128, 128)] = up_back.astype(BF16)
        pre = dot(tokens, Wd[:, :, :, :, pl.ds(512, 128)].reshape(experts * rb, 128))
        turned = pltpu.roll(pre, 64, axis=1)
        low_ = low(2 * n_tok)
        upstream = H[:, :, pl.ds(256, 128)].reshape(2 * n_tok, 128).astype(F32)
        gate_back, up_back = backs(jnp.where(low_, pre, turned), jnp.where(low_, turned, pre), upstream)
        Dback[:, pl.ds(512, 128)] = jnp.where(low_, gate_back, up_back).astype(BF16)

    def dense_share(t_):
        block = Wd[t_ // 2, pl.ds(lax.rem(t_, 2) * (X // 2), X // 2)]
        return nt(Dback[...], block.reshape(dq, 640))

    d_sib, d_x = {}, {}

    def dense_back():
        for dyh in (1, 0):
            yh_ = chip(0, dyh)[1]
            Dsib_s[dyh] = dense_share(yh_ * 2 + 1 - c).astype(BF16).reshape(2, n_tok, dq)
            d_sib[dyh] = push(Dsib_s.at[dyh], Dsib_r.at[dyh], sibling)
        for dyh in (1, 0):
            yh_ = chip(0, dyh)[1]
            part = dense_share(yh_ * 2 + c)
            d_sib[dyh].wait_recv()
            total = part.reshape(2, n_tok, dq) + Dsib_r[dyh].astype(F32)
            Dx_s[dyh] = total.astype(BF16)
            for dyl in (0, 1):
                if dyl or dyh:
                    yl_ = chip(dyl, dyh)[0]
                    d_x[dyl, dyh] = push(Dx_s.at[dyh, yl_], Dx_r.at[dyl, dyh], dev(yl_, x, z, yh_, c))
            if not dyh:
                Dtot[...] = total

    z_back = []
    for h in range(CHUNKS):
        for dyl, dyh in others:
            e_x[h, dyl, dyh].wait_recv()
        R2[h, yl] = (Etot[h, yl] + Ex_r[h, 0, 1].astype(F32)).astype(BF16)
        R2[h, 1 - yl] = (Ex_r[h, 1, 0].astype(F32) + Ex_r[h, 1, 1].astype(F32)).astype(BF16)
        Z2[h] = dot(perms[2], stack(R2[h].reshape(slots, dc))).astype(BF16).reshape(Z, 2 * X * ten, w)
        z_back.append([push(Z2.at[h, zr(d)], ZB.at[h, z], dev(yl, x, zr(d), yh, c)) for d in z_order])
        ZB[h, z] = Z2[h, z]
        if h == CHUNKS // 2 - 1:
            dense_forward()
            dense_back()
    x_back = []
    for h in range(CHUNKS):
        for copy in z_back[h]:
            copy.wait_recv()
        ZBp[h] = spread(dot(perms[3], ZB[h].reshape(rows, w))).astype(BF16).reshape(X, Z * ten, dc)
        x_back.append([push(ZBp.at[h, xr(d)], XB.at[h, x], dev(yl, xr(d), z, yh, c)) for d in x_order])
        XB[h, x] = ZBp[h, x]

    for dyl, dyh in others:
        d_x[dyl, dyh].wait_recv()
    out_sum = (
        res[...].astype(F32) + Dtot[yl] + Dx_r[0, 1].astype(F32) + Dx_r[1, 0].astype(F32) + Dx_r[1, 1].astype(F32)
    )
    Dtot[0] = out_sum
    down = jnp.concatenate([code, weight, jnp.zeros((124, 128), F32)], axis=0).T
    hots = [jnp.where(key_lane[0:1, :] == down[:, k:k + 1], 1.0, 0.0).astype(BF16) for k in range(2)]
    for h in range(CHUNKS):
        for copy in x_back[h]:
            copy.wait_recv()
        returned = XB[h].reshape(slots, dc)
        total = Dtot[0, :, pl.ds(h * dc, dc)]
        for k in range(2):
            total = total + down[:, 2 + k:3 + k] * dot(hots[k], returned)
        out[:, pl.ds(h * dc, dc)] = total.astype(BF16)
    for copy in pending:
        copy.wait_send()


SERVICE = {"x3": 1, "z1": 1, "z3": 1, "f0": 1, "y1": 1, "f2": 1, "y3": 1, "f3": 1, "b0": 1, "b1": 1}
N_SEMS = 256


def run_kernel(tok, ids, slot, kept, gate_w, dg, du, dh, eg, eu, eh, res):
    experts, slots, ten, rows = sizes()
    half = slots // 2
    n_tok, dq = tok.shape
    d = dq * 4
    dc = dq // CHUNKS
    w = dc // 2
    rb = dg.shape[0]
    table, key_lane = tables()
    vm = pl.BlockSpec(memory_space=pltpu.VMEM)
    hbm = pl.BlockSpec(memory_space=pl.ANY)
    V = pltpu.VMEM
    C = CHUNKS
    wide = eg.shape[1] * 2
    eg, eu = (m.reshape(4, C, dc, m.shape[1]) for m in (eg, eu))
    return pl.pallas_call(
        kernel,
        out_shape=jax.ShapeDtypeStruct((n_tok, dq), BF16),
        in_specs=[vm] * 8 + [hbm, hbm] + [vm] * 4,
        out_specs=vm,
        scratch_shapes=[
            V((2, n_tok, d), BF16),
            V((2, rb, 640), BF16),
            V((2, n_tok, 384), BF16),
            V((2, n_tok, 384), BF16),
            V((2, X, Z, rb, 640), BF16),
            V((4, C, dc, wide), BF16),
            V((4, rows, rows), BF16),
            V((C, X, Z * ten, dc), BF16),
            V((C, X, Z * ten, dc), BF16),
            V((C, Z, 2 * X * ten, w), BF16),
            V((C, Z, 2 * X * ten, w), BF16),
            V((C, 2, half, dc), BF16),
            V((C, 2, half, 4 * dc), BF16),
            V((slots, wide), F32),
            V((slots, wide), BF16),
            V((C, 2, slots, dc), BF16),
            V((C, 2, slots, dc), BF16),
            V((C, 2, 2, half, dc), BF16),
            V((C, 2, 2, half, dc), BF16),
            V((C, 2, half, dc), F32),
            V((C, 2, half, dc), BF16),
            V((C, Z, 2 * X * ten, w), BF16),
            V((C, Z, 2 * X * ten, w), BF16),
            V((C, X, Z * ten, dc), BF16),
            V((C, X, Z * ten, dc), BF16),
            V((2 * n_tok, 640), BF16),
            V((2, 2, n_tok, dq), BF16),
            V((2, 2, n_tok, dq), BF16),
            V((2, 2, n_tok, dq), BF16),
            V((2, 2, n_tok, dq), BF16),
            V((2, n_tok, dq), F32),
            pltpu.SemaphoreType.DMA((N_SEMS,)),
            pltpu.SemaphoreType.DMA((N_SEMS,)),
            pltpu.SemaphoreType.DMA((16,)),
        ],
        compiler_params=pltpu.CompilerParams(
            collective_id=0, has_side_effects=True, vmem_limit_bytes=60 * 1024 * 1024
        ),
    )(
        tok, ids, slot, kept, gate_w, dg, du, dh, eg, eu, eh, res,
        jnp.asarray(table), jnp.asarray(key_lane),
    )


def body(
    tokens,
    residual_grad,
    dense_hidden,
    dense_gate,
    dense_up,
    expert_gate,
    expert_up,
    expert_hidden,
    expert_ids,
    slot_index,
    kept_mask,
    gate_weights,
):
    return run_kernel(
        tokens, expert_ids.T, slot_index.T, kept_mask.T, gate_weights.T, dense_gate, dense_up, dense_hidden,
        expert_gate[0], expert_up[0], expert_hidden[0], residual_grad,
    )


def solution(mesh):
    both = P("expert", "tensor")
    rows = P("expert", None)
    last = P("expert", None, "tensor")
    placed = (both, both, both, both, both, last, last, last, rows, rows, rows, rows)
    return jax.shard_map(body, mesh=mesh, in_specs=placed, out_specs=both, check_vma=False)
```
